512 devices in a mesh: dom: 32 (over x, y, core), cls: 16 (over z).
Axes of the slice: x: 4, y: 4, z: 16, core: 2. Of those that a mesh axis runs over, the one named last changes fastest.
Arguments:
- images: bfloat16 [16384, 128, 128], P(('dom', 'cls')), may hold values from -6 to 6
- class_ids: int32 [16384], P(('dom', 'cls')), may hold values from 0 to 255, as said below
- shifts: int32 [16384, 2], P(('dom', 'cls')), may hold values from -16 to 16
- defocus_bins: int32 [16384], P(('dom', 'cls')), may hold values from 0 to 31
- defocus: float32 [32], replicated, may hold values from 20 to 200
- regular: float32 [128, 128], replicated, may hold values from 1 to 32
Outputs:
- class_avg: float32 [256, 128, 128], P('cls')
The draws below stay inside these ranges and needn't reach their ends.
Inputs may be any that keep to these rules, and one draw needn't show every extreme that they name: `class_ids`: the owner of class k is k // 16. Among the 32 particles of one device exactly 8 have classes of one owner, and every other owner has at most 2 of them, exactly 2 for some; all devices with the same dom index have that same most loaded owner.
All inputs are finite; a program needn't handle non-finite values.
Results may differ from the reference program's by a relative error of at most 0.0055.
Values may be sent and summed in bfloat16 or wider, within the bound.
No kernel may reach another device: no remote copies, remote signals or barrier semaphores. Data moves between devices by JAX's collectives and lax.ppermute only.
A program may use at most 64 MiB of HBM per device.

```python
import math
import jax
import jax.numpy as jnp
from jax import lax

SIDE = 128
STACK = 32
OWNED = 16
BINS = 32
CAPACITY = 8
PARTICLES = 16384
CLASSES = 256
N_DOM = 32
N_CLS = 16


def draw_class_ids(key, part):
    subkeys = jax.random.split(jax.random.fold_in(key, 71), 5)
    heavy_owner = jax.random.randint(subkeys[0], (N_DOM, 1, 1), 0, N_CLS)
    scores = jax.random.randint(subkeys[1], (N_DOM, N_CLS, N_CLS - 1), 0, 1 << 20) * (N_CLS - 1) + jnp.arange(N_CLS - 1, dtype=jnp.int32)
    others = jnp.argsort(scores, axis=-1).astype(jnp.int32)
    slot_ids = jnp.arange(STACK, dtype=jnp.int32)
    column = jnp.maximum(slot_ids - CAPACITY, 0) % (N_CLS - 1)
    column = jnp.broadcast_to(column, (N_DOM, N_CLS, STACK)).astype(jnp.int32)
    picked = jnp.take_along_axis(others, column, axis=-1)
    owner_of = jnp.where(slot_ids[None, None, :] < CAPACITY, heavy_owner, (heavy_owner + 1 + picked) % N_CLS)
    order_scores = jax.random.randint(subkeys[3], (N_DOM, N_CLS, STACK), 0, 1 << 20) * STACK + slot_ids
    order_ids = jnp.argsort(order_scores, axis=-1).astype(jnp.int32)
    owner_of = jnp.take_along_axis(owner_of, order_ids, axis=-1)
    within = jax.random.randint(subkeys[4], (N_DOM, N_CLS, STACK), 0, OWNED)
    return (owner_of * OWNED + within).reshape(-1).astype(jnp.int32)


def set_ends(entries, stream_key, least, high):
    spot = [jax.random.randint(jax.random.fold_in(stream_key, axis), (), 0, length) for axis, length in enumerate(entries.shape)]
    longest = entries.shape.index(max(entries.shape))
    neighbour = spot[:longest] + [(spot[longest] + 1) % entries.shape[longest]] + spot[longest + 1:]
    return entries.at[tuple(spot)].set(least).at[tuple(neighbour)].set(high)


def block_levels(own_key, dims, shards, smallest, high):
    level, own = 1.0, jax.random.fold_in(own_key, 6)
    for position, blocks in shards:
        heights = jnp.exp(jax.random.uniform(jax.random.fold_in(own, position), (blocks,), jnp.float32, smallest / len(shards), high / len(shards)))
        level = level * jnp.repeat(heights, dims[position] // blocks).reshape([-1 if axis == position else 1 for axis in range(len(dims))])
    return level


def noise(rng, dims, spread, bound, pieces=(), kind=jnp.bfloat16):
    drawn = jax.random.normal(rng, dims, jnp.float32) * spread
    if len(pieces) > 0:
        drawn = block_levels(rng, dims, pieces, -0.22, 0.18) * drawn
    return jnp.clip(drawn, min=-bound, max=bound).astype(kind)


def setup_inputs(seed: int = 0) -> dict:
    arg_keys = jax.random.split(jax.random.key(seed), 7)
    return {
        "images": noise(arg_keys[0], (PARTICLES, SIDE, SIDE), 1.0, 6.0, ((0, 512),)),
        "class_ids": draw_class_ids(jax.random.fold_in(arg_keys[6], 71), 0),
        "shifts": set_ends(jax.random.randint(arg_keys[2], (PARTICLES, 2), -(SIDE // 8), SIDE // 8 + 1), jax.random.fold_in(arg_keys[2], 1), -(SIDE // 8), (SIDE // 8 + 1) - 1).astype(jnp.int32),
        "defocus_bins": set_ends(jax.random.randint(arg_keys[3], (PARTICLES,), 0, BINS), jax.random.fold_in(arg_keys[3], 1), 0, BINS - 1).astype(jnp.int32),
        "defocus": jnp.clip(jnp.exp(jax.random.uniform(arg_keys[4], (BINS,), jnp.float32, math.log(20.0), math.log(200.0))), 20.0, 200.0),
        "regular": jnp.clip(jnp.exp(jax.random.uniform(arg_keys[5], (SIDE, SIDE), jnp.float32, math.log(1.0), math.log(32.0))), 1.0, 32.0),
    }


PHASE = 0.1
EPSILON = 1e-05

def hartley_tables(image_side):
    indices = jnp.arange(image_side, dtype=jnp.int32)
    product = indices[:, None] * indices[None, :] % image_side
    angles = product.astype(jnp.float32) * (2.0 * math.pi / image_side)
    return (jnp.cos(angles), jnp.sin(angles))

def frequency_squared(image_side):
    indices = jnp.arange(image_side, dtype=jnp.int32)
    signed = jnp.where(indices < image_side // 2, indices, indices - image_side).astype(jnp.float32) / image_side
    return signed[:, None] * signed[:, None] + signed[None, :] * signed[None, :]

def lookup(bins, defocus):
    levels = jnp.arange(defocus.shape[0], dtype=jnp.int32)
    return lax.optimization_barrier(jnp.sum(jnp.where(bins[:, None] == levels[None, :], defocus[None, :], 0.0), axis=1))

def weigh_block(pictures, offsets, bins, defocus):
    count_rows = pictures.shape[0]
    indices = jnp.arange(SIDE, dtype=jnp.int32)

    def move(picture, offset):
        return picture[(indices - offset[0]) % SIDE][:, (indices - offset[1]) % SIDE]
    shifted = jax.vmap(move)(pictures, offsets)
    cosine, sine_table = hartley_tables(SIDE)
    factor = 1.0 / math.sqrt(SIDE)
    right_table = (jnp.concatenate([cosine + sine_table, cosine - sine_table], axis=1) * factor).astype(jnp.bfloat16)
    left_table = (jnp.stack([cosine, sine_table]) * factor).astype(jnp.bfloat16)
    halves = jnp.dot(shifted.reshape(count_rows * SIDE, SIDE), right_table, preferred_element_type=jnp.float32).astype(jnp.bfloat16)
    halves = halves.reshape(count_rows, SIDE, 2, SIDE)
    spectrum = jnp.einsum('kux,pxkv->puv', left_table.astype(jnp.float32), halves.astype(jnp.float32), precision=lax.Precision.HIGHEST)
    ctf_values = -jnp.sin(lookup(bins, defocus)[:, None, None] * frequency_squared(SIDE)[None] + PHASE)
    weighted = (ctf_values * spectrum).astype(jnp.bfloat16)
    return (weighted.reshape(count_rows, SIDE * SIDE), ctf_values.reshape(count_rows, SIDE * SIDE))

def invert(average):
    classes_here = average.shape[0]
    cosine, sine_table = hartley_tables(SIDE)
    right_table = jnp.concatenate([cosine + sine_table, cosine - sine_table], axis=1)
    left_table = jnp.stack([cosine, sine_table])
    halves = jnp.dot(average.reshape(classes_here * SIDE, SIDE), right_table, precision=lax.Precision.HIGHEST)
    halves = halves.reshape(classes_here, SIDE, 2, SIDE)
    real_image = jnp.einsum('kux,pxkv->puv', left_table, halves, precision=lax.Precision.HIGHEST)
    power_mean = lax.optimization_barrier(jnp.mean(real_image * real_image, axis=(1, 2), keepdims=True))
    return real_image / jnp.sqrt(power_mean + EPSILON)

def reference(images, class_ids, shifts, defocus_bins, defocus, regular):
    group_size = PARTICLES // N_DOM
    blocks = (images.reshape(N_DOM, group_size, SIDE, SIDE), class_ids.reshape(N_DOM, group_size), shifts.reshape(N_DOM, group_size, 2), defocus_bins.reshape(N_DOM, group_size))

    def accumulate(totals, block_data):
        pictures, labels, offsets, bins = block_data
        weighted, ctf_values = weigh_block(pictures, offsets, bins, defocus)
        numerator = totals[0] + jax.ops.segment_sum(weighted.astype(jnp.float32), labels, num_segments=CLASSES)
        denominator = totals[1] + jax.ops.segment_sum(ctf_values * ctf_values, labels, num_segments=CLASSES)
        return ((numerator, denominator), None)
    start = (jnp.zeros((CLASSES, SIDE * SIDE), jnp.float32), jnp.zeros((CLASSES, SIDE * SIDE), jnp.float32))
    totals, unused = lax.scan(accumulate, start, blocks)
    average = totals[0] / (totals[1] + regular.reshape(1, SIDE * SIDE))
    return invert(average)
```

```python
import functools
import math

import jax
import jax.numpy as jnp
import ml_dtypes
import numpy as np
from jax import lax
from jax.experimental import pallas as pl
from jax.experimental.pallas import tpu as pltpu
from jax.sharding import PartitionSpec as P

SIDE = 128
STACK = 32
OWNED = 16
CLASSES = 256
N_DOM = 32
N_CLS = 16
BINS = 32
REACH = 16
PER = SIDE // N_DOM
ROWS = PER * STACK + 16
WIDE = PER * SIDE
LIMIT = 56 * 1024 * 1024
PHASE = 0.1
EPSILON = 1e-05

VMEM = pl.BlockSpec(memory_space=pltpu.VMEM)
SMEM = pl.BlockSpec(memory_space=pltpu.SMEM)
PARAMS = pltpu.CompilerParams(vmem_limit_bytes=LIMIT)


def hartley_tables():
    indices = np.arange(SIDE)
    angles = ((indices[:, None] * indices[None, :]) % SIDE).astype(np.float32)
    angles = angles * np.float32(2.0 * math.pi / SIDE)
    return np.cos(angles).astype(np.float32), np.sin(angles).astype(np.float32)


def forward_tables():
    cosine, sine = hartley_tables()
    factor = np.float32(1.0 / math.sqrt(SIDE))
    right = (np.concatenate([cosine + sine, cosine - sine], axis=1) * factor).astype(ml_dtypes.bfloat16)
    left_cos = (cosine * factor).astype(ml_dtypes.bfloat16)
    left_sin = (sine * factor).astype(ml_dtypes.bfloat16)
    indices = np.arange(SIDE)
    rights, lefts = [], []
    for shift in range(-REACH, REACH + 1):
        moved = (indices + shift) % SIDE
        rights.append(right[moved])
        lefts.append(np.concatenate([left_cos[:, moved], left_sin[:, moved]], axis=1))
    return np.stack(rights), np.stack(lefts)


def split(table):
    high = table.astype(ml_dtypes.bfloat16)
    low = (table - high.astype(np.float32)).astype(ml_dtypes.bfloat16)
    return high, low


def inverse_tables():
    cosine, sine = hartley_tables()
    left_high, left_low = split(np.concatenate([cosine, sine], axis=0))
    left = np.concatenate([left_high, left_low], axis=1)
    right_high, right_low = split(np.concatenate([cosine + sine, cosine - sine], axis=0))
    return left, right_high, right_low


def forward_kernel(shifts, bins, images, rights, lefts, ctf, tags, out, spectra):
    def particle(p, carry):
        right = rights[shifts[p, 1] + REACH]
        left = lefts[shifts[p, 0] + REACH]
        halves = jnp.dot(images[p], right, preferred_element_type=jnp.float32).astype(jnp.bfloat16)
        stacked = jnp.concatenate([halves[:, :SIDE], halves[:, SIDE:]], axis=0)
        spectrum = jnp.dot(left, stacked, preferred_element_type=jnp.float32)
        start = pl.multiple_of(p * SIDE, SIDE)
        spectra[pl.ds(start, SIDE), :] = ctf[bins[p]] * spectrum
        return carry

    lax.fori_loop(0, STACK, particle, 0, unroll=4)
    for u in range(SIDE):
        j, d = u // N_DOM, u % N_DOM
        row = spectra[pl.ds(u, STACK, stride=SIDE), :]
        out[d, j * STACK : (j + 1) * STACK, :] = row.astype(jnp.bfloat16)
    tile = tags[...]
    for d in range(N_DOM):
        out[d, PER * STACK :, :] = tile


def gather_kernel(arrived, out):
    together = N_DOM // 8
    sums = jnp.zeros((CLASSES, WIDE), jnp.float32)
    counts = jnp.zeros((CLASSES, SIDE), jnp.float32)
    classes = lax.broadcasted_iota(jnp.int32, (CLASSES, SIDE), 0).astype(jnp.float32)
    levels = lax.broadcasted_iota(jnp.int32, (SIDE, SIDE), 0)
    levels = jnp.where(levels < 2 * BINS, levels % BINS, -1).astype(jnp.float32)
    for pair in range(4):
        picks, blocks = [], []
        for g in (2 * pair, 2 * pair + 1):
            tag = sum(
                arrived[g * together + k, PER * STACK :, :].astype(jnp.float32)
                for k in range(together)
            )
            pick = jnp.where(classes == tag[0:1, :], 1.0, 0.0).astype(jnp.bfloat16)
            level = jnp.where(levels == tag[1:2, :], 1.0, 0.0).astype(jnp.bfloat16)
            counts += lax.dot_general(
                pick, level, (((1,), (1,)), ((), ())), preferred_element_type=jnp.float32
            )
            picks.append(pick)
            blocks.append(
                jnp.concatenate(
                    [
                        jnp.concatenate(
                            [
                                arrived[g * together + k, j * STACK : (j + 1) * STACK, :]
                                for k in range(together)
                            ],
                            axis=0,
                        )
                        for j in range(PER)
                    ],
                    axis=1,
                )
            )
        sums += jnp.dot(
            jnp.concatenate(picks, axis=1),
            jnp.concatenate(blocks, axis=0),
            preferred_element_type=jnp.float32,
        )
    lanes = lax.broadcasted_iota(jnp.int32, (CLASSES, SIDE), 1)
    high = jnp.floor(counts * (1.0 / 32.0))
    digits = jnp.where(lanes < BINS, counts - 32.0 * high, high)
    out[:, :WIDE] = sums.astype(jnp.bfloat16)
    out[:, WIDE:] = digits.astype(jnp.bfloat16)


def average_kernel(arrived, squares, regular, out):
    total = arrived[0].astype(jnp.float32)
    for z in range(1, N_CLS):
        total += arrived[z].astype(jnp.float32)
    denominator = jnp.dot(
        total[:, WIDE:],
        squares[...],
        precision=lax.Precision.HIGHEST,
        preferred_element_type=jnp.float32,
    )
    average = total[:, :WIDE] / (denominator + regular[...])
    average = jnp.concatenate(
        [average[:, j * SIDE : (j + 1) * SIDE] for j in range(PER)], axis=0
    ).astype(jnp.bfloat16)
    for d in range(N_DOM):
        out[d] = average


def invert_kernel(arrived, left, right, out, rows):
    count = PER * OWNED
    for d in range(N_DOM):
        rows[d * count : (d + 1) * count, :] = arrived[d].astype(jnp.float32)

    def picture(k):
        parts = [rows[pl.ds(j * OWNED + k, N_DOM, stride=count), :] for j in range(PER)]
        return jnp.concatenate(parts, axis=0).astype(jnp.bfloat16)

    for k in range(0, OWNED, 2):
        both = jnp.concatenate([picture(k), picture(k + 1)], axis=1)
        first = jnp.dot(
            left[...], jnp.concatenate([both, both], axis=0), preferred_element_type=jnp.float32
        ).astype(jnp.bfloat16)
        for i in range(2):
            half = first[:, i * SIDE : (i + 1) * SIDE]
            wide = jnp.concatenate([half[:SIDE], half[SIDE:]], axis=1)
            real = jnp.dot(wide, right[...], preferred_element_type=jnp.float32)
            power = jnp.sum(real * real, axis=0, keepdims=True)
            power = jnp.sum(power, axis=1, keepdims=True) * (1.0 / (SIDE * SIDE))
            out[k + i] = real * (1.0 / jnp.sqrt(power + EPSILON))


def body(images, class_ids, shifts, defocus_bins, defocus, regular):
    dom = lax.axis_index("dom")
    indices = np.arange(SIDE)
    signed = np.where(indices < SIDE // 2, indices, indices - SIDE).astype(np.float32) / SIDE
    squared = jnp.asarray((signed * signed).astype(np.float32))
    along = defocus[:, None] * squared[None, :]
    sin_u, cos_u = jnp.sin(along + PHASE), jnp.cos(along + PHASE)
    sin_v, cos_v = jnp.sin(along), jnp.cos(along)
    ctf = -(sin_u[:, :, None] * cos_v[:, None, :] + cos_u[:, :, None] * sin_v[:, None, :])

    def own(table):
        return lax.dynamic_slice_in_dim(
            table.reshape(*table.shape[:-1], PER, N_DOM), dom, 1, axis=-1
        )

    mine = own(sin_u) * cos_v[:, None, :] + own(cos_u) * sin_v[:, None, :]
    mine = (mine * mine).reshape(BINS, WIDE)
    squares = jnp.concatenate(
        [mine, 32.0 * mine, jnp.zeros((SIDE - 2 * BINS, WIDE), jnp.float32)], axis=0
    )
    own_regular = lax.dynamic_slice_in_dim(
        regular.reshape(PER, N_DOM, SIDE), dom, 1, axis=1
    ).reshape(1, WIDE)

    lanes = jnp.arange(SIDE, dtype=jnp.int32)
    here = (lanes // STACK == dom % 4)[None, :]
    numbers = jnp.stack([class_ids, defocus_bins]).astype(jnp.bfloat16)
    tags = jnp.where(here, jnp.tile(numbers, (1, 4)), jnp.bfloat16(0))
    tags = jnp.concatenate([tags, jnp.zeros((14, SIDE), jnp.bfloat16)], axis=0)

    rights, lefts = forward_tables()
    payload = pl.pallas_call(
        forward_kernel,
        out_shape=jax.ShapeDtypeStruct((N_DOM, ROWS, SIDE), jnp.bfloat16),
        in_specs=[SMEM, SMEM, VMEM, VMEM, VMEM, VMEM, VMEM],
        out_specs=VMEM,
        scratch_shapes=[pltpu.VMEM((STACK * SIDE, SIDE), jnp.float32)],
        compiler_params=PARAMS,
    )(shifts, defocus_bins, images, jnp.asarray(rights), jnp.asarray(lefts), ctf, tags)

    arrived = lax.all_to_all(payload, "dom", split_axis=0, concat_axis=0, tiled=True)
    sums = pl.pallas_call(
        gather_kernel,
        out_shape=jax.ShapeDtypeStruct((CLASSES, WIDE + SIDE), jnp.bfloat16),
        in_specs=[VMEM],
        out_specs=VMEM,
        compiler_params=PARAMS,
    )(arrived)

    arrived = lax.all_to_all(
        sums.reshape(N_CLS, OWNED, WIDE + SIDE), "cls", split_axis=0, concat_axis=0, tiled=True
    )
    averages = pl.pallas_call(
        average_kernel,
        out_shape=jax.ShapeDtypeStruct((N_DOM, PER * OWNED, SIDE), jnp.bfloat16),
        in_specs=[VMEM, VMEM, VMEM],
        out_specs=VMEM,
        compiler_params=PARAMS,
    )(arrived, squares, own_regular)

    arrived = lax.all_to_all(averages, "dom", split_axis=0, concat_axis=0, tiled=True)
    left, right, _ = inverse_tables()
    return pl.pallas_call(
        invert_kernel,
        out_shape=jax.ShapeDtypeStruct((OWNED, SIDE, SIDE), jnp.float32),
        in_specs=[VMEM, VMEM, VMEM],
        out_specs=VMEM,
        scratch_shapes=[pltpu.VMEM((N_DOM * PER * OWNED, SIDE), jnp.float32)],
        compiler_params=PARAMS,
    )(arrived, jnp.asarray(left), jnp.asarray(right))


def solution(mesh):
    in_specs = (
        P(("dom", "cls"), None, None),
        P(("dom", "cls")),
        P(("dom", "cls"), None),
        P(("dom", "cls")),
        P(),
        P(),
    )
    return jax.shard_map(
        body, mesh=mesh, in_specs=in_specs, out_specs=P("cls", None, None), check_vma=False
    )
```

```python
import math

import jax
import jax.numpy as jnp
import ml_dtypes
import numpy as np
from jax import lax
from jax.experimental import pallas as pl
from jax.experimental.pallas import tpu as pltpu
from jax.sharding import PartitionSpec as P

SIDE = 128
STACK = 32
OWNED = 16
CLASSES = 256
N_DOM = 32
N_CLS = 16
BINS = 32
REACH = 16
PER = SIDE // N_DOM
ROWS = PER * STACK + 16
WIDE = PER * SIDE
GROUP = 16
APART = SIDE + 8
SPREAD = PER * OWNED + 8
PHASE = 0.1
EPSILON = 1e-05

VMEM = pl.BlockSpec(memory_space=pltpu.VMEM)
HBM = pl.BlockSpec(memory_space=pl.ANY)
SMEM = pl.BlockSpec(memory_space=pltpu.SMEM)
ALL = pltpu.CompilerParams(vmem_limit_bytes=60 * 1024 * 1024)
PARAMS = pltpu.CompilerParams(vmem_limit_bytes=16 * 1024 * 1024)


def hartley_tables():
    indices = np.arange(SIDE)
    angles = ((indices[:, None] * indices[None, :]) % SIDE).astype(np.float32)
    angles = angles * np.float32(2.0 * math.pi / SIDE)
    return np.cos(angles).astype(np.float32), np.sin(angles).astype(np.float32)


def forward_tables():
    cosine, sine = hartley_tables()
    factor = np.float32(1.0 / math.sqrt(SIDE))
    right = (np.concatenate([cosine + sine, cosine - sine], axis=1) * factor).astype(ml_dtypes.bfloat16)
    left = (np.concatenate([cosine, sine], axis=1) * factor).astype(ml_dtypes.bfloat16)
    return right, left


def split(table):
    high = table.astype(ml_dtypes.bfloat16)
    low = (table - high.astype(np.float32)).astype(ml_dtypes.bfloat16)
    return high, low


def inverse_tables():
    cosine, sine = hartley_tables()
    left_high, left_low = split(np.concatenate([cosine, sine], axis=0))
    left = np.concatenate([left_high, left_low], axis=1)
    right_high, right_low = split(np.concatenate([cosine + sine, cosine - sine], axis=0))
    return left, right_high, right_low


def forward_kernel(
    shifts, bins, class_ids, defocus, images, right, left, out, pictures, moved, spectra, trig, sems
):
    def picture_copy(g):
        part = pl.ds(g * GROUP, GROUP)
        return pltpu.make_async_copy(images.at[part], pictures.at[part], sems.at[g])

    for g in range(STACK // GROUP):
        picture_copy(g).start()

    lane = lax.broadcasted_iota(jnp.int32, (SIDE, SIDE), 1)
    line = lax.broadcasted_iota(jnp.int32, (SIDE, SIDE), 0)

    def squared(index):
        signed = jnp.where(index < SIDE // 2, index, index - SIDE).astype(jnp.float32) * (1.0 / SIDE)
        return signed * signed

    by_lane = jnp.zeros((1, SIDE), jnp.float32)
    by_line = jnp.zeros((BINS, SIDE), jnp.float32)
    for b in range(BINS):
        level = defocus[b]
        by_lane = jnp.where(lane[:1] == b, level, by_lane)
        by_line = jnp.where(line[:BINS] == b, level, by_line)
    angles = jnp.concatenate(
        [squared(line) * by_lane + PHASE, squared(lane[:BINS]) * by_line], axis=0
    )
    trig[0] = jnp.sin(angles)
    trig[1] = jnp.cos(angles)

    tag_class = jnp.zeros((1, SIDE), jnp.int32)
    tag_bin = jnp.zeros((1, SIDE), jnp.int32)
    first = lax.rem(lax.axis_index("dom"), 4) * STACK
    for p in range(STACK):
        tag_class = jnp.where(lane[:1] == first + p, class_ids[p], tag_class)
        tag_bin = jnp.where(lane[:1] == first + p, bins[p], tag_bin)
    tile = jnp.where(line[:16] == 0, tag_class, jnp.where(line[:16] == 1, tag_bin, 0))
    tile = tile.astype(jnp.float32).astype(jnp.bfloat16)
    for d in range(N_DOM):
        out[d, PER * STACK :, :] = tile

    def group(g, carry):
        picture_copy(g).wait()
        shifted = []
        for i in range(GROUP):
            p = g * GROUP + i
            picture = pictures[p].astype(jnp.float32)
            picture = pltpu.roll(picture, lax.rem(shifts[1, p] + SIDE, SIDE), axis=1)
            moved[i, REACH : REACH + SIDE, :] = picture
            moved[i, :REACH, :] = picture[SIDE - REACH :]
            moved[i, REACH + SIDE :, :] = picture[:REACH]
            shifted.append(moved[i, pl.ds(REACH - shifts[0, p], SIDE), :].astype(jnp.bfloat16))
        halves = jnp.dot(
            jnp.concatenate(shifted, axis=0), right[...], preferred_element_type=jnp.float32
        ).astype(jnp.bfloat16)
        for i in range(0, GROUP, 2):
            one = halves[i * SIDE : (i + 1) * SIDE]
            two = halves[(i + 1) * SIDE : (i + 2) * SIDE]
            both = jnp.concatenate(
                [
                    jnp.concatenate([one[:, :SIDE], two[:, :SIDE]], axis=1),
                    jnp.concatenate([one[:, SIDE:], two[:, SIDE:]], axis=1),
                ],
                axis=0,
            )
            spectrum = jnp.dot(left[...], both, preferred_element_type=jnp.float32)
            for k in range(2):
                p = g * GROUP + i + k
                level = bins[p]
                which = jnp.full((SIDE, SIDE), level, jnp.int32)
                sin_u = jnp.take_along_axis(trig[0, :SIDE], which, axis=1)
                cos_u = jnp.take_along_axis(trig[1, :SIDE], which, axis=1)
                sin_v = trig[0, pl.ds(SIDE + level, 1), :]
                cos_v = trig[1, pl.ds(SIDE + level, 1), :]
                ctf = -(sin_u * cos_v + cos_u * sin_v)
                start = pl.multiple_of(p * APART, 8)
                spectra[pl.ds(start, SIDE), :] = ctf * spectrum[:, k * SIDE : (k + 1) * SIDE]
        return carry

    lax.fori_loop(0, STACK // GROUP, group, 0)
    for u in range(SIDE):
        j, d = u // N_DOM, u % N_DOM
        row = spectra[pl.ds(u, STACK, stride=APART), :]
        out[d, j * STACK : (j + 1) * STACK, :] = row.astype(jnp.bfloat16)


def gather_kernel(arrived, out):
    together = SIDE // STACK
    classes = lax.broadcasted_iota(jnp.int32, (CLASSES, SIDE), 0).astype(jnp.float32)
    levels = (lax.broadcasted_iota(jnp.int32, (SIDE, SIDE), 0) % BINS).astype(jnp.float32)
    picks, lots, blocks = [], [], []
    for g in range(N_DOM // together):
        members = range(g * together, (g + 1) * together)
        tag = sum(arrived[s, PER * STACK :, :].astype(jnp.float32) for s in members)
        picks.append(jnp.where(classes == tag[0:1, :], 1.0, 0.0).astype(jnp.bfloat16))
        lots.append(jnp.where(levels == tag[1:2, :], 1.0, 0.0).astype(jnp.bfloat16))
        parts = [
            jnp.concatenate([arrived[s, j * STACK : (j + 1) * STACK, :] for s in members], axis=0)
            for j in range(PER)
        ]
        blocks.append(jnp.concatenate(parts, axis=1))
    pick = jnp.concatenate(picks, axis=1)
    sums = jnp.dot(pick, jnp.concatenate(blocks, axis=0), preferred_element_type=jnp.float32)
    counts = lax.dot_general(
        pick,
        jnp.concatenate(lots, axis=1),
        (((1,), (1,)), ((), ())),
        preferred_element_type=jnp.float32,
    )
    lanes = lax.broadcasted_iota(jnp.int32, (CLASSES, SIDE), 1)
    high = jnp.floor(counts * (1.0 / 32.0))
    digits = jnp.where(lanes % (2 * BINS) < BINS, counts - 32.0 * high, high)
    out[:, :WIDE] = sums.astype(jnp.bfloat16)
    out[:, WIDE:] = digits.astype(jnp.bfloat16)


def average_kernel(arrived, squares, regular, out):
    total = arrived[0].astype(jnp.float32)
    for z in range(1, N_CLS):
        total += arrived[z].astype(jnp.float32)
    lanes = lax.broadcasted_iota(jnp.int32, (OWNED, SIDE), 1)
    even = lanes % (2 * BINS) < BINS
    digits = total[:, WIDE:]
    ahead = pltpu.roll(digits, SIDE - BINS, axis=1)
    behind = pltpu.roll(digits, BINS, axis=1)
    counts = jnp.where(even, digits + 32.0 * ahead, behind + 32.0 * digits)
    high = jnp.floor(counts * (1.0 / 128.0))
    digits = jnp.where(even, counts - 128.0 * high, high).astype(jnp.bfloat16)
    denominator = jnp.dot(digits, squares[...], preferred_element_type=jnp.float32)
    average = total[:, :WIDE] / (denominator + regular[...])
    average = jnp.concatenate(
        [average[:, j * SIDE : (j + 1) * SIDE] for j in range(PER)], axis=0
    ).astype(jnp.bfloat16)
    for d in range(N_DOM):
        out[d] = average


def invert_kernel(arrived, left, right, out, rows):
    count = PER * OWNED
    for d in range(N_DOM):
        rows[d * SPREAD : d * SPREAD + count, :] = arrived[d].astype(jnp.float32)

    def picture(k):
        parts = [rows[pl.ds(j * OWNED + k, N_DOM, stride=SPREAD), :] for j in range(PER)]
        return jnp.concatenate(parts, axis=0).astype(jnp.bfloat16)

    for k in range(0, OWNED, 2):
        both = jnp.concatenate([picture(k), picture(k + 1)], axis=1)
        first = jnp.dot(
            left[...], jnp.concatenate([both, both], axis=0), preferred_element_type=jnp.float32
        ).astype(jnp.bfloat16)
        wide = jnp.concatenate(
            [
                jnp.concatenate([first[:SIDE, :SIDE], first[SIDE:, :SIDE]], axis=1),
                jnp.concatenate([first[:SIDE, SIDE:], first[SIDE:, SIDE:]], axis=1),
            ],
            axis=0,
        )
        pair = jnp.dot(wide, right[...], preferred_element_type=jnp.float32)
        for i in range(2):
            real = pair[i * SIDE : (i + 1) * SIDE]
            power = jnp.sum(real * real, axis=0, keepdims=True)
            power = jnp.sum(power, axis=1, keepdims=True) * (1.0 / (SIDE * SIDE))
            out[k + i] = real * (1.0 / jnp.sqrt(power + EPSILON))


def body(images, class_ids, shifts, defocus_bins, defocus, regular):
    dom = lax.axis_index("dom")
    indices = np.arange(SIDE)
    signed = np.where(indices < SIDE // 2, indices, indices - SIDE).astype(np.float32) / SIDE
    squared = jnp.asarray((signed * signed).astype(np.float32))
    along = defocus[:, None] * squared[None, :]
    sin_u, cos_u = jnp.sin(along + PHASE), jnp.cos(along + PHASE)
    sin_v, cos_v = jnp.sin(along), jnp.cos(along)

    def own(table):
        return lax.dynamic_slice_in_dim(
            table.reshape(*table.shape[:-1], PER, N_DOM), dom, 1, axis=-1
        )

    mine = own(sin_u) * cos_v[:, None, :] + own(cos_u) * sin_v[:, None, :]
    mine = (mine * mine).reshape(BINS, WIDE)
    high = mine.astype(jnp.bfloat16)
    low = (mine - high.astype(jnp.float32)).astype(jnp.bfloat16)
    squares = jnp.concatenate([high, 128 * high, low, 128 * low], axis=0)
    own_regular = lax.dynamic_slice_in_dim(
        regular.reshape(PER, N_DOM, SIDE), dom, 1, axis=1
    ).reshape(1, WIDE)

    right, left = forward_tables()
    payload = pl.pallas_call(
        forward_kernel,
        out_shape=jax.ShapeDtypeStruct((N_DOM, ROWS, SIDE), jnp.bfloat16),
        in_specs=[SMEM, SMEM, SMEM, SMEM, HBM, VMEM, VMEM],
        out_specs=VMEM,
        scratch_shapes=[
            pltpu.VMEM((STACK, SIDE, SIDE), jnp.bfloat16),
            pltpu.VMEM((GROUP, SIDE + 2 * REACH, SIDE), jnp.float32),
            pltpu.VMEM((STACK * APART, SIDE), jnp.float32),
            pltpu.VMEM((2, SIDE + BINS, SIDE), jnp.float32),
            pltpu.SemaphoreType.DMA((STACK // GROUP,)),
        ],
        compiler_params=ALL,
    )(shifts.T, defocus_bins, class_ids, defocus, images, jnp.asarray(right), jnp.asarray(left))

    arrived = lax.all_to_all(payload, "dom", split_axis=0, concat_axis=0, tiled=True)
    sums = pl.pallas_call(
        gather_kernel,
        out_shape=jax.ShapeDtypeStruct((CLASSES, WIDE + SIDE), jnp.bfloat16),
        in_specs=[VMEM],
        out_specs=VMEM,
        compiler_params=PARAMS,
    )(arrived)

    arrived = lax.all_to_all(
        sums.reshape(N_CLS, OWNED, WIDE + SIDE), "cls", split_axis=0, concat_axis=0, tiled=True
    )
    averages = pl.pallas_call(
        average_kernel,
        out_shape=jax.ShapeDtypeStruct((N_DOM, PER * OWNED, SIDE), jnp.bfloat16),
        in_specs=[VMEM, VMEM, VMEM],
        out_specs=VMEM,
        compiler_params=PARAMS,
    )(arrived, squares, own_regular)

    arrived = lax.all_to_all(averages, "dom", split_axis=0, concat_axis=0, tiled=True)
    left, right, _ = inverse_tables()
    return pl.pallas_call(
        invert_kernel,
        out_shape=jax.ShapeDtypeStruct((OWNED, SIDE, SIDE), jnp.float32),
        in_specs=[VMEM, VMEM, VMEM],
        out_specs=VMEM,
        scratch_shapes=[pltpu.VMEM((N_DOM * SPREAD, SIDE), jnp.float32)],
        compiler_params=PARAMS,
    )(arrived, jnp.asarray(left), jnp.asarray(right))


def solution(mesh):
    in_specs = (
        P(("dom", "cls"), None, None),
        P(("dom", "cls")),
        P(("dom", "cls"), None),
        P(("dom", "cls")),
        P(),
        P(),
    )
    return jax.shard_map(
        body, mesh=mesh, in_specs=in_specs, out_specs=P("cls", None, None), check_vma=False
    )
```

```python
import math

import jax
import jax.numpy as jnp
import ml_dtypes
import numpy as np
from jax import lax
from jax.experimental import pallas as pl
from jax.experimental.pallas import tpu as pltpu
from jax.sharding import PartitionSpec as P

SIDE = 128
STACK = 32
OWNED = 16
CLASSES = 256
N_DOM = 32
N_CLS = 16
BINS = 32
REACH = 16
PAIR = 2
TEAM = N_DOM * PAIR
FAR = N_CLS // PAIR
NEAR = OWNED * PAIR
PER = SIDE // TEAM
BLOCK = PER * STACK
TAGS = 8
WIDE = PER * SIDE
GROUP = 16
APART = SIDE + 8
SPREAD = PER * OWNED + 8
PHASE = 0.1
EPSILON = 1e-05

VMEM = pl.BlockSpec(memory_space=pltpu.VMEM)
HBM = pl.BlockSpec(memory_space=pl.ANY)
SMEM = pl.BlockSpec(memory_space=pltpu.SMEM)
ALL = pltpu.CompilerParams(vmem_limit_bytes=60 * 1024 * 1024)
PARAMS = pltpu.CompilerParams(vmem_limit_bytes=16 * 1024 * 1024)


def hartley_tables():
    indices = np.arange(SIDE)
    angles = ((indices[:, None] * indices[None, :]) % SIDE).astype(np.float32)
    angles = angles * np.float32(2.0 * math.pi / SIDE)
    return np.cos(angles).astype(np.float32), np.sin(angles).astype(np.float32)


def forward_tables():
    cosine, sine = hartley_tables()
    factor = np.float32(1.0 / math.sqrt(SIDE))
    right = (np.concatenate([cosine + sine, cosine - sine], axis=1) * factor).astype(ml_dtypes.bfloat16)
    left = (np.concatenate([cosine, sine], axis=1) * factor).astype(ml_dtypes.bfloat16)
    return right, left


def split(table):
    high = table.astype(ml_dtypes.bfloat16)
    low = (table - high.astype(np.float32)).astype(ml_dtypes.bfloat16)
    return high, low


def inverse_tables():
    cosine, sine = hartley_tables()
    left_high, left_low = split(np.concatenate([cosine, sine], axis=0))
    left = np.concatenate([left_high, left_low], axis=1)
    right_high, right_low = split(np.concatenate([cosine + sine, cosine - sine], axis=0))
    return left, right_high, right_low


def member_index():
    return lax.axis_index("dom") * PAIR + lax.rem(lax.axis_index("cls"), PAIR)


def forward_kernel(
    shifts, bins, class_ids, defocus, images, right, left, out, pictures, moved, spectra, trig, sems
):
    def picture_copy(g):
        part = pl.ds(g * GROUP, GROUP)
        return pltpu.make_async_copy(images.at[part], pictures.at[part], sems.at[g])

    for g in range(STACK // GROUP):
        picture_copy(g).start()

    lane = lax.broadcasted_iota(jnp.int32, (SIDE, SIDE), 1)
    line = lax.broadcasted_iota(jnp.int32, (SIDE, SIDE), 0)

    def squared(index):
        signed = jnp.where(index < SIDE // 2, index, index - SIDE).astype(jnp.float32) * (1.0 / SIDE)
        return signed * signed

    by_lane = jnp.zeros((1, SIDE), jnp.float32)
    by_line = jnp.zeros((BINS, SIDE), jnp.float32)
    for b in range(BINS):
        level = defocus[b]
        by_lane = jnp.where(lane[:1] == b, level, by_lane)
        by_line = jnp.where(line[:BINS] == b, level, by_line)
    angles = jnp.concatenate(
        [squared(line) * by_lane + PHASE, squared(lane[:BINS]) * by_line], axis=0
    )
    trig[0] = jnp.sin(angles)
    trig[1] = jnp.cos(angles)

    tag_class = jnp.zeros((1, SIDE), jnp.int32)
    tag_bin = jnp.zeros((1, SIDE), jnp.int32)
    first = lax.rem(member_index(), SIDE // STACK) * STACK
    for p in range(STACK):
        tag_class = jnp.where(lane[:1] == first + p, class_ids[p], tag_class)
        tag_bin = jnp.where(lane[:1] == first + p, bins[p], tag_bin)
    tile = jnp.where(line[:TAGS] == 0, tag_class, jnp.where(line[:TAGS] == 1, tag_bin, 0))
    tile = tile.astype(jnp.float32).astype(jnp.bfloat16)
    for m in range(TEAM):
        out[m, BLOCK:, :] = tile

    def group(g, carry):
        picture_copy(g).wait()
        shifted = []
        for i in range(GROUP):
            p = g * GROUP + i
            picture = pictures[p].astype(jnp.float32)
            picture = pltpu.roll(picture, lax.rem(shifts[1, p] + SIDE, SIDE), axis=1)
            moved[i, REACH : REACH + SIDE, :] = picture
            moved[i, :REACH, :] = picture[SIDE - REACH :]
            moved[i, REACH + SIDE :, :] = picture[:REACH]
            shifted.append(moved[i, pl.ds(REACH - shifts[0, p], SIDE), :].astype(jnp.bfloat16))
        halves = jnp.dot(
            jnp.concatenate(shifted, axis=0), right[...], preferred_element_type=jnp.float32
        ).astype(jnp.bfloat16)
        for i in range(0, GROUP, 2):
            one = halves[i * SIDE : (i + 1) * SIDE]
            two = halves[(i + 1) * SIDE : (i + 2) * SIDE]
            both = jnp.concatenate(
                [
                    jnp.concatenate([one[:, :SIDE], two[:, :SIDE]], axis=1),
                    jnp.concatenate([one[:, SIDE:], two[:, SIDE:]], axis=1),
                ],
                axis=0,
            )
            spectrum = jnp.dot(left[...], both, preferred_element_type=jnp.float32)
            for k in range(2):
                p = g * GROUP + i + k
                level = bins[p]
                which = jnp.full((SIDE, SIDE), level, jnp.int32)
                sin_u = jnp.take_along_axis(trig[0, :SIDE], which, axis=1)
                cos_u = jnp.take_along_axis(trig[1, :SIDE], which, axis=1)
                sin_v = trig[0, pl.ds(SIDE + level, 1), :]
                cos_v = trig[1, pl.ds(SIDE + level, 1), :]
                ctf = -(sin_u * cos_v + cos_u * sin_v)
                start = pl.multiple_of(p * APART, 8)
                spectra[pl.ds(start, SIDE), :] = ctf * spectrum[:, k * SIDE : (k + 1) * SIDE]
        return carry

    lax.fori_loop(0, STACK // GROUP, group, 0)
    for u in range(SIDE):
        j, m = u // TEAM, u % TEAM
        row = spectra[pl.ds(u, STACK, stride=APART), :]
        out[m, j * STACK : (j + 1) * STACK, :] = row.astype(jnp.bfloat16)


def gather_kernel(arrived, out):
    together = SIDE // STACK
    classes = lax.broadcasted_iota(jnp.int32, (CLASSES, SIDE), 0).astype(jnp.float32)
    levels = (lax.broadcasted_iota(jnp.int32, (SIDE, SIDE), 0) % BINS).astype(jnp.float32)
    picks, lots, blocks = [], [], []
    for g in range(TEAM // together):
        members = range(g * together, (g + 1) * together)
        tag = sum(arrived[s, BLOCK:, :].astype(jnp.float32) for s in members)
        picks.append(jnp.where(classes == tag[0:1, :], 1.0, 0.0).astype(jnp.bfloat16))
        lots.append(jnp.where(levels == tag[1:2, :], 1.0, 0.0).astype(jnp.bfloat16))
        parts = [
            jnp.concatenate([arrived[s, j * STACK : (j + 1) * STACK, :] for s in members], axis=0)
            for j in range(PER)
        ]
        blocks.append(jnp.concatenate(parts, axis=1))
    pick = jnp.concatenate(picks, axis=1)
    sums = jnp.dot(pick, jnp.concatenate(blocks, axis=0), preferred_element_type=jnp.float32)
    counts = lax.dot_general(
        pick,
        jnp.concatenate(lots, axis=1),
        (((1,), (1,)), ((), ())),
        preferred_element_type=jnp.float32,
    )
    counts = counts.reshape(FAR, PAIR, OWNED, SIDE)
    lanes = lax.broadcasted_iota(jnp.int32, (FAR, OWNED, SIDE), 2)
    counts = jnp.where(lanes < SIDE // 2, counts[:, 0], counts[:, 1])
    high = jnp.floor(counts * (1.0 / 32.0))
    digits = jnp.where(lanes % (2 * BINS) < BINS, counts - 32.0 * high, high)
    sums = sums.astype(jnp.bfloat16)
    for j in range(PER):
        out[:, j * NEAR : (j + 1) * NEAR, :] = sums[:, j * SIDE : (j + 1) * SIDE].reshape(
            FAR, NEAR, SIDE
        )
    out[:, PER * NEAR :, :] = digits.astype(jnp.bfloat16)


def average_kernel(arrived, squares, regular, out):
    total = arrived[0].astype(jnp.float32)
    for z in range(1, FAR):
        total += arrived[z].astype(jnp.float32)
    lanes = lax.broadcasted_iota(jnp.int32, (OWNED, SIDE), 1)
    even = lanes % (2 * BINS) < BINS
    digits = total[PER * NEAR :]
    ahead = pltpu.roll(digits, SIDE - BINS, axis=1)
    behind = pltpu.roll(digits, BINS, axis=1)
    counts = jnp.where(even, digits + 32.0 * ahead, behind + 32.0 * digits)
    other = pltpu.roll(counts, SIDE // 2, axis=1)
    near = lanes < SIDE // 2
    counts = jnp.concatenate(
        [jnp.where(near, counts, other), jnp.where(near, other, counts)], axis=0
    )
    even = jnp.concatenate([even, even], axis=0)
    high = jnp.floor(counts * (1.0 / 128.0))
    digits = jnp.where(even, counts - 128.0 * high, high).astype(jnp.bfloat16)
    denominator = jnp.dot(digits, squares[...], preferred_element_type=jnp.float32)
    denominator = denominator + regular[...]
    averages = [
        (
            total[j * NEAR : (j + 1) * NEAR] / denominator[:, j * SIDE : (j + 1) * SIDE]
        ).astype(jnp.bfloat16)
        for j in range(PER)
    ]
    for i in range(PAIR):
        block = jnp.concatenate(
            [average[i * OWNED : (i + 1) * OWNED] for average in averages], axis=0
        )
        for d in range(N_DOM):
            out[d * PAIR + i] = block


def invert_kernel(arrived, left, right, out, rows):
    count = PER * OWNED
    for m in range(TEAM):
        rows[m * SPREAD : m * SPREAD + count, :] = arrived[m].astype(jnp.float32)

    def picture(k):
        parts = [rows[pl.ds(j * OWNED + k, TEAM, stride=SPREAD), :] for j in range(PER)]
        return jnp.concatenate(parts, axis=0).astype(jnp.bfloat16)

    for k in range(0, OWNED, 2):
        both = jnp.concatenate([picture(k), picture(k + 1)], axis=1)
        first = jnp.dot(
            left[...], jnp.concatenate([both, both], axis=0), preferred_element_type=jnp.float32
        ).astype(jnp.bfloat16)
        wide = jnp.concatenate(
            [
                jnp.concatenate([first[:SIDE, :SIDE], first[SIDE:, :SIDE]], axis=1),
                jnp.concatenate([first[:SIDE, SIDE:], first[SIDE:, SIDE:]], axis=1),
            ],
            axis=0,
        )
        pair = jnp.dot(wide, right[...], preferred_element_type=jnp.float32)
        for i in range(2):
            real = pair[i * SIDE : (i + 1) * SIDE]
            power = jnp.sum(real * real, axis=0, keepdims=True)
            power = jnp.sum(power, axis=1, keepdims=True) * (1.0 / (SIDE * SIDE))
            out[k + i] = real * (1.0 / jnp.sqrt(power + EPSILON))


TEAMS = [
    [d * N_CLS + t * PAIR + i for d in range(N_DOM) for i in range(PAIR)] for t in range(FAR)
]
LINES = [[i + PAIR * t for t in range(FAR)] for i in range(PAIR)]


def exchange(array, axes, groups):
    return lax.all_to_all(
        array, axes, split_axis=0, concat_axis=0, tiled=True, axis_index_groups=groups
    )


def body(images, class_ids, shifts, defocus_bins, defocus, regular):
    member = member_index()
    indices = np.arange(SIDE)
    signed = np.where(indices < SIDE // 2, indices, indices - SIDE).astype(np.float32) / SIDE
    squared = jnp.asarray((signed * signed).astype(np.float32))
    along = defocus[:, None] * squared[None, :]
    sin_u, cos_u = jnp.sin(along + PHASE), jnp.cos(along + PHASE)
    sin_v, cos_v = jnp.sin(along), jnp.cos(along)

    def own(table):
        return lax.dynamic_slice_in_dim(
            table.reshape(*table.shape[:-1], PER, TEAM), member, 1, axis=-1
        )

    mine = own(sin_u) * cos_v[:, None, :] + own(cos_u) * sin_v[:, None, :]
    mine = (mine * mine).reshape(BINS, WIDE)
    high = mine.astype(jnp.bfloat16)
    low = (mine - high.astype(jnp.float32)).astype(jnp.bfloat16)
    squares = jnp.concatenate([high, 128 * high, low, 128 * low], axis=0)
    own_regular = lax.dynamic_slice_in_dim(
        regular.reshape(PER, TEAM, SIDE), member, 1, axis=1
    ).reshape(1, WIDE)

    right, left = forward_tables()
    payload = pl.pallas_call(
        forward_kernel,
        out_shape=jax.ShapeDtypeStruct((TEAM, BLOCK + TAGS, SIDE), jnp.bfloat16),
        in_specs=[SMEM, SMEM, SMEM, SMEM, HBM, VMEM, VMEM],
        out_specs=VMEM,
        scratch_shapes=[
            pltpu.VMEM((STACK, SIDE, SIDE), jnp.bfloat16),
            pltpu.VMEM((GROUP, SIDE + 2 * REACH, SIDE), jnp.float32),
            pltpu.VMEM((STACK * APART, SIDE), jnp.float32),
            pltpu.VMEM((2, SIDE + BINS, SIDE), jnp.float32),
            pltpu.SemaphoreType.DMA((STACK // GROUP,)),
        ],
        compiler_params=ALL,
    )(shifts.T, defocus_bins, class_ids, defocus, images, jnp.asarray(right), jnp.asarray(left))

    arrived = exchange(payload, ("dom", "cls"), TEAMS)
    sums = pl.pallas_call(
        gather_kernel,
        out_shape=jax.ShapeDtypeStruct((FAR, PER * NEAR + OWNED, SIDE), jnp.bfloat16),
        in_specs=[VMEM],
        out_specs=VMEM,
        compiler_params=PARAMS,
    )(arrived)

    arrived = exchange(sums, "cls", LINES)
    averages = pl.pallas_call(
        average_kernel,
        out_shape=jax.ShapeDtypeStruct((TEAM, PER * OWNED, SIDE), jnp.bfloat16),
        in_specs=[VMEM, VMEM, VMEM],
        out_specs=VMEM,
        compiler_params=PARAMS,
    )(arrived, squares, own_regular)

    arrived = exchange(averages, ("dom", "cls"), TEAMS)
    left, right, _ = inverse_tables()
    return pl.pallas_call(
        invert_kernel,
        out_shape=jax.ShapeDtypeStruct((OWNED, SIDE, SIDE), jnp.float32),
        in_specs=[VMEM, VMEM, VMEM],
        out_specs=VMEM,
        scratch_shapes=[pltpu.VMEM((TEAM * SPREAD, SIDE), jnp.float32)],
        compiler_params=PARAMS,
    )(arrived, jnp.asarray(left), jnp.asarray(right))


def solution(mesh):
    in_specs = (
        P(("dom", "cls"), None, None),
        P(("dom", "cls")),
        P(("dom", "cls"), None),
        P(("dom", "cls")),
        P(),
        P(),
    )
    return jax.shard_map(
        body, mesh=mesh, in_specs=in_specs, out_specs=P("cls", None, None), check_vma=False
    )
```

```python
import math

import jax
import jax.numpy as jnp
import ml_dtypes
import numpy as np
from jax import lax
from jax.experimental import pallas as pl
from jax.experimental.pallas import tpu as pltpu
from jax.sharding import PartitionSpec as P

SIDE = 128
STACK = 32
OWNED = 16
CLASSES = 256
N_DOM = 32
N_CLS = 16
BINS = 32
REACH = 16
PAIR = 2
TEAM = N_DOM * PAIR
FAR = N_CLS // PAIR
NEAR = OWNED * PAIR
PER = SIDE // TEAM
BLOCK = PER * STACK
TAGS = 8
TURN = 5
START = 21
WIDE = PER * SIDE
GROUP = 16
APART = SIDE + 8
SPREAD = PER * OWNED + 8
PHASE = 0.1
EPSILON = 1e-05

VMEM = pl.BlockSpec(memory_space=pltpu.VMEM)
HBM = pl.BlockSpec(memory_space=pl.ANY)
SMEM = pl.BlockSpec(memory_space=pltpu.SMEM)
ALL = pltpu.CompilerParams(vmem_limit_bytes=60 * 1024 * 1024)
PARAMS = pltpu.CompilerParams(vmem_limit_bytes=16 * 1024 * 1024)


def hartley_tables():
    indices = np.arange(SIDE)
    angles = ((indices[:, None] * indices[None, :]) % SIDE).astype(np.float32)
    angles = angles * np.float32(2.0 * math.pi / SIDE)
    return np.cos(angles).astype(np.float32), np.sin(angles).astype(np.float32)


def forward_tables():
    cosine, sine = hartley_tables()
    factor = np.float32(1.0 / math.sqrt(SIDE))
    right = (np.concatenate([cosine + sine, cosine - sine], axis=1) * factor).astype(ml_dtypes.bfloat16)
    left = (np.concatenate([cosine, sine], axis=1) * factor).astype(ml_dtypes.bfloat16)
    return right, left


def split(table):
    high = table.astype(ml_dtypes.bfloat16)
    low = (table - high.astype(np.float32)).astype(ml_dtypes.bfloat16)
    return high, low


def inverse_tables():
    cosine, sine = hartley_tables()
    left_high, left_low = split(np.concatenate([cosine, sine], axis=0))
    left = np.concatenate([left_high, left_low], axis=1)
    right_high, right_low = split(np.concatenate([cosine + sine, cosine - sine], axis=0))
    return left, right_high, right_low


def member_index():
    return lax.rem(lax.axis_index("dom") + N_DOM - START, N_DOM) * PAIR + lax.rem(lax.axis_index("cls"), PAIR)


def forward_kernel(
    shifts, bins, class_ids, defocus, images, right, left, out, pictures, moved, spectra, trig, sems
):
    def picture_copy(g):
        part = pl.ds(g * GROUP, GROUP)
        return pltpu.make_async_copy(images.at[part], pictures.at[part], sems.at[g])

    for g in range(STACK // GROUP):
        picture_copy(g).start()

    lane = lax.broadcasted_iota(jnp.int32, (SIDE, SIDE), 1)
    line = lax.broadcasted_iota(jnp.int32, (SIDE, SIDE), 0)

    def squared(index):
        signed = jnp.where(index < SIDE // 2, index, index - SIDE).astype(jnp.float32) * (1.0 / SIDE)
        return signed * signed

    by_lane = jnp.zeros((1, SIDE), jnp.float32)
    by_line = jnp.zeros((BINS, SIDE), jnp.float32)
    for b in range(BINS):
        level = defocus[b]
        by_lane = jnp.where(lane[:1] == b, level, by_lane)
        by_line = jnp.where(line[:BINS] == b, level, by_line)
    angles = jnp.concatenate(
        [squared(line) * by_lane + PHASE, squared(lane[:BINS]) * by_line], axis=0
    )
    trig[0] = jnp.sin(angles)
    trig[1] = jnp.cos(angles)

    tag_class = jnp.zeros((1, SIDE), jnp.int32)
    tag_bin = jnp.zeros((1, SIDE), jnp.int32)
    first = lax.rem(member_index(), SIDE // STACK) * STACK
    for p in range(STACK):
        tag_class = jnp.where(lane[:1] == first + p, class_ids[p], tag_class)
        tag_bin = jnp.where(lane[:1] == first + p, bins[p], tag_bin)
    tile = jnp.where(line[:TAGS] == 0, tag_class, jnp.where(line[:TAGS] == 1, tag_bin, 0))
    tile = tile.astype(jnp.float32).astype(jnp.bfloat16)
    for m in range(TEAM):
        out[m, BLOCK:, :] = tile

    def group(g, carry):
        picture_copy(g).wait()
        shifted = []
        for i in range(GROUP):
            p = g * GROUP + i
            picture = pictures[p].astype(jnp.float32)
            picture = pltpu.roll(picture, lax.rem(shifts[1, p] + SIDE, SIDE), axis=1)
            moved[i, REACH : REACH + SIDE, :] = picture
            moved[i, :REACH, :] = picture[SIDE - REACH :]
            moved[i, REACH + SIDE :, :] = picture[:REACH]
            shifted.append(moved[i, pl.ds(REACH - shifts[0, p], SIDE), :].astype(jnp.bfloat16))
        halves = jnp.dot(
            jnp.concatenate(shifted, axis=0), right[...], preferred_element_type=jnp.float32
        ).astype(jnp.bfloat16)
        for i in range(0, GROUP, 2):
            one = halves[i * SIDE : (i + 1) * SIDE]
            two = halves[(i + 1) * SIDE : (i + 2) * SIDE]
            both = jnp.concatenate(
                [
                    jnp.concatenate([one[:, :SIDE], two[:, :SIDE]], axis=1),
                    jnp.concatenate([one[:, SIDE:], two[:, SIDE:]], axis=1),
                ],
                axis=0,
            )
            spectrum = jnp.dot(left[...], both, preferred_element_type=jnp.float32)
            for k in range(2):
                p = g * GROUP + i + k
                level = bins[p]
                which = jnp.full((SIDE, SIDE), level, jnp.int32)
                sin_u = jnp.take_along_axis(trig[0, :SIDE], which, axis=1)
                cos_u = jnp.take_along_axis(trig[1, :SIDE], which, axis=1)
                sin_v = trig[0, pl.ds(SIDE + level, 1), :]
                cos_v = trig[1, pl.ds(SIDE + level, 1), :]
                ctf = -(sin_u * cos_v + cos_u * sin_v)
                start = pl.multiple_of(p * APART, 8)
                spectra[pl.ds(start, SIDE), :] = ctf * spectrum[:, k * SIDE : (k + 1) * SIDE]
        return carry

    lax.fori_loop(0, STACK // GROUP, group, 0)
    for u in range(SIDE):
        j, m = u // TEAM, u % TEAM
        row = spectra[pl.ds(u, STACK, stride=APART), :]
        out[m, j * STACK : (j + 1) * STACK, :] = row.astype(jnp.bfloat16)


def gather_kernel(arrived, out):
    together = SIDE // STACK
    classes = lax.broadcasted_iota(jnp.int32, (CLASSES, SIDE), 0).astype(jnp.float32)
    levels = (lax.broadcasted_iota(jnp.int32, (SIDE, SIDE), 0) % BINS).astype(jnp.float32)
    picks, lots, blocks = [], [], []
    for g in range(TEAM // together):
        members = range(g * together, (g + 1) * together)
        tag = sum(arrived[s, BLOCK:, :].astype(jnp.float32) for s in members)
        picks.append(jnp.where(classes == tag[0:1, :], 1.0, 0.0).astype(jnp.bfloat16))
        lots.append(jnp.where(levels == tag[1:2, :], 1.0, 0.0).astype(jnp.bfloat16))
        parts = [
            jnp.concatenate([arrived[s, j * STACK : (j + 1) * STACK, :] for s in members], axis=0)
            for j in range(PER)
        ]
        blocks.append(jnp.concatenate(parts, axis=1))
    pick = jnp.concatenate(picks, axis=1)
    sums = jnp.dot(pick, jnp.concatenate(blocks, axis=0), preferred_element_type=jnp.float32)
    counts = lax.dot_general(
        pick,
        jnp.concatenate(lots, axis=1),
        (((1,), (1,)), ((), ())),
        preferred_element_type=jnp.float32,
    )
    counts = counts.reshape(FAR, PAIR, OWNED, SIDE)
    lanes = lax.broadcasted_iota(jnp.int32, (FAR, OWNED, SIDE), 2)
    counts = jnp.where(lanes < SIDE // 2, counts[:, 0], counts[:, 1])
    high = jnp.floor(counts * (1.0 / 32.0))
    digits = jnp.where(lanes % (2 * BINS) < BINS, counts - 32.0 * high, high)
    sums = sums.astype(jnp.bfloat16)
    digits = digits.astype(jnp.bfloat16)
    for t in range(FAR):
        far = (t + TURN) % FAR
        for j in range(PER):
            out[t, j * NEAR : (j + 1) * NEAR, :] = sums[
                far * NEAR : (far + 1) * NEAR, j * SIDE : (j + 1) * SIDE
            ]
        out[t, PER * NEAR :, :] = digits[far]


def average_kernel(arrived, squares, regular, out):
    total = arrived[0].astype(jnp.float32)
    for z in range(1, FAR):
        total += arrived[z].astype(jnp.float32)
    lanes = lax.broadcasted_iota(jnp.int32, (OWNED, SIDE), 1)
    even = lanes % (2 * BINS) < BINS
    digits = total[PER * NEAR :]
    ahead = pltpu.roll(digits, SIDE - BINS, axis=1)
    behind = pltpu.roll(digits, BINS, axis=1)
    counts = jnp.where(even, digits + 32.0 * ahead, behind + 32.0 * digits)
    other = pltpu.roll(counts, SIDE // 2, axis=1)
    near = lanes < SIDE // 2
    counts = jnp.concatenate(
        [jnp.where(near, counts, other), jnp.where(near, other, counts)], axis=0
    )
    even = jnp.concatenate([even, even], axis=0)
    high = jnp.floor(counts * (1.0 / 128.0))
    digits = jnp.where(even, counts - 128.0 * high, high).astype(jnp.bfloat16)
    denominator = jnp.dot(digits, squares[...], preferred_element_type=jnp.float32)
    denominator = denominator + regular[...]
    averages = [
        (
            total[j * NEAR : (j + 1) * NEAR] / denominator[:, j * SIDE : (j + 1) * SIDE]
        ).astype(jnp.bfloat16)
        for j in range(PER)
    ]
    for i in range(PAIR):
        block = jnp.concatenate(
            [average[i * OWNED : (i + 1) * OWNED] for average in averages], axis=0
        )
        for d in range(N_DOM):
            out[d * PAIR + i] = block


def invert_kernel(arrived, left, right, out, rows):
    count = PER * OWNED
    for m in range(TEAM):
        rows[m * SPREAD : m * SPREAD + count, :] = arrived[m].astype(jnp.float32)

    def picture(k):
        parts = [rows[pl.ds(j * OWNED + k, TEAM, stride=SPREAD), :] for j in range(PER)]
        return jnp.concatenate(parts, axis=0).astype(jnp.bfloat16)

    for k in range(0, OWNED, 2):
        both = jnp.concatenate([picture(k), picture(k + 1)], axis=1)
        first = jnp.dot(
            left[...], jnp.concatenate([both, both], axis=0), preferred_element_type=jnp.float32
        ).astype(jnp.bfloat16)
        wide = jnp.concatenate(
            [
                jnp.concatenate([first[:SIDE, :SIDE], first[SIDE:, :SIDE]], axis=1),
                jnp.concatenate([first[:SIDE, SIDE:], first[SIDE:, SIDE:]], axis=1),
            ],
            axis=0,
        )
        pair = jnp.dot(wide, right[...], preferred_element_type=jnp.float32)
        for i in range(2):
            real = pair[i * SIDE : (i + 1) * SIDE]
            power = jnp.sum(real * real, axis=0, keepdims=True)
            power = jnp.sum(power, axis=1, keepdims=True) * (1.0 / (SIDE * SIDE))
            out[k + i] = real * (1.0 / jnp.sqrt(power + EPSILON))


TEAMS = [
    [
        (d + START) % N_DOM * N_CLS + t * PAIR + i for d in range(N_DOM) for i in range(PAIR)
    ]
    for t in range(FAR)
]
LINES = [[i + PAIR * ((t + TURN) % FAR) for t in range(FAR)] for i in range(PAIR)]


def exchange(array, axes, groups):
    return lax.all_to_all(
        array, axes, split_axis=0, concat_axis=0, tiled=True, axis_index_groups=groups
    )


def body(images, class_ids, shifts, defocus_bins, defocus, regular):
    member = member_index()
    indices = np.arange(SIDE)
    signed = np.where(indices < SIDE // 2, indices, indices - SIDE).astype(np.float32) / SIDE
    squared = jnp.asarray((signed * signed).astype(np.float32))
    along = defocus[:, None] * squared[None, :]
    sin_u, cos_u = jnp.sin(along + PHASE), jnp.cos(along + PHASE)
    sin_v, cos_v = jnp.sin(along), jnp.cos(along)

    def own(table):
        return lax.dynamic_slice_in_dim(
            table.reshape(*table.shape[:-1], PER, TEAM), member, 1, axis=-1
        )

    mine = own(sin_u) * cos_v[:, None, :] + own(cos_u) * sin_v[:, None, :]
    mine = (mine * mine).reshape(BINS, WIDE)
    high = mine.astype(jnp.bfloat16)
    low = (mine - high.astype(jnp.float32)).astype(jnp.bfloat16)
    squares = jnp.concatenate([high, 128 * high, low, 128 * low], axis=0)
    own_regular = lax.dynamic_slice_in_dim(
        regular.reshape(PER, TEAM, SIDE), member, 1, axis=1
    ).reshape(1, WIDE)

    right, left = forward_tables()
    payload = pl.pallas_call(
        forward_kernel,
        out_shape=jax.ShapeDtypeStruct((TEAM, BLOCK + TAGS, SIDE), jnp.bfloat16),
        in_specs=[SMEM, SMEM, SMEM, SMEM, HBM, VMEM, VMEM],
        out_specs=VMEM,
        scratch_shapes=[
            pltpu.VMEM((STACK, SIDE, SIDE), jnp.bfloat16),
            pltpu.VMEM((GROUP, SIDE + 2 * REACH, SIDE), jnp.float32),
            pltpu.VMEM((STACK * APART, SIDE), jnp.float32),
            pltpu.VMEM((2, SIDE + BINS, SIDE), jnp.float32),
            pltpu.SemaphoreType.DMA((STACK // GROUP,)),
        ],
        compiler_params=ALL,
    )(shifts.T, defocus_bins, class_ids, defocus, images, jnp.asarray(right), jnp.asarray(left))

    arrived = exchange(payload, ("dom", "cls"), TEAMS)
    sums = pl.pallas_call(
        gather_kernel,
        out_shape=jax.ShapeDtypeStruct((FAR, PER * NEAR + OWNED, SIDE), jnp.bfloat16),
        in_specs=[VMEM],
        out_specs=VMEM,
        compiler_params=PARAMS,
    )(arrived)

    arrived = exchange(sums, "cls", LINES)
    averages = pl.pallas_call(
        average_kernel,
        out_shape=jax.ShapeDtypeStruct((TEAM, PER * OWNED, SIDE), jnp.bfloat16),
        in_specs=[VMEM, VMEM, VMEM],
        out_specs=VMEM,
        compiler_params=PARAMS,
    )(arrived, squares, own_regular)

    arrived = exchange(averages, ("dom", "cls"), TEAMS)
    left, right, _ = inverse_tables()
    return pl.pallas_call(
        invert_kernel,
        out_shape=jax.ShapeDtypeStruct((OWNED, SIDE, SIDE), jnp.float32),
        in_specs=[VMEM, VMEM, VMEM],
        out_specs=VMEM,
        scratch_shapes=[pltpu.VMEM((TEAM * SPREAD, SIDE), jnp.float32)],
        compiler_params=PARAMS,
    )(arrived, jnp.asarray(left), jnp.asarray(right))


def solution(mesh):
    in_specs = (
        P(("dom", "cls"), None, None),
        P(("dom", "cls")),
        P(("dom", "cls"), None),
        P(("dom", "cls")),
        P(),
        P(),
    )
    return jax.shard_map(
        body, mesh=mesh, in_specs=in_specs, out_specs=P("cls", None, None), check_vma=False
    )
```

```python
import math

import jax
import jax.numpy as jnp
import ml_dtypes
import numpy as np
from jax import lax
from jax.experimental import pallas as pl
from jax.experimental.pallas import tpu as pltpu
from jax.sharding import PartitionSpec as P

SIDE = 128
STACK = 32
OWNED = 16
CLASSES = 256
N_DOM = 32
N_CLS = 16
BINS = 32
REACH = 16
PAIR = 2
TEAM = N_DOM * PAIR
FAR = N_CLS // PAIR
NEAR = OWNED * PAIR
PER = SIDE // TEAM
BLOCK = PER * STACK
TAGS = 8
ORDER = (5, 1, 6, 2, 7, 3, 0, 4)
START = 21
LAST = 21
WIDE = PER * SIDE
GROUP = 16
SLAB = 16
APART = SIDE + 8
SPREAD = PER * OWNED + 8
PHASE = 0.1
EPSILON = 1e-05

VMEM = pl.BlockSpec(memory_space=pltpu.VMEM)
HBM = pl.BlockSpec(memory_space=pl.ANY)
SMEM = pl.BlockSpec(memory_space=pltpu.SMEM)
ALL = pltpu.CompilerParams(vmem_limit_bytes=60 * 1024 * 1024)
PARAMS = pltpu.CompilerParams(vmem_limit_bytes=16 * 1024 * 1024)


def hartley_tables():
    indices = np.arange(SIDE)
    angles = ((indices[:, None] * indices[None, :]) % SIDE).astype(np.float32)
    angles = angles * np.float32(2.0 * math.pi / SIDE)
    return np.cos(angles).astype(np.float32), np.sin(angles).astype(np.float32)


def forward_tables():
    cosine, sine = hartley_tables()
    factor = np.float32(1.0 / math.sqrt(SIDE))
    right = (np.concatenate([cosine + sine, cosine - sine], axis=1) * factor).astype(ml_dtypes.bfloat16)
    left = (np.concatenate([cosine, sine], axis=1) * factor).astype(ml_dtypes.bfloat16)
    return right, left


def split(table):
    high = table.astype(ml_dtypes.bfloat16)
    low = (table - high.astype(np.float32)).astype(ml_dtypes.bfloat16)
    return high, low


def inverse_tables():
    cosine, sine = hartley_tables()
    left_high, left_low = split(np.concatenate([cosine, sine], axis=0))
    left = np.concatenate([left_high, left_low], axis=1)
    right_high, right_low = split(np.concatenate([cosine + sine, cosine - sine], axis=0))
    return left, right_high, right_low


def member_index():
    return lax.rem(lax.axis_index("dom") + N_DOM - START, N_DOM) * PAIR + lax.rem(lax.axis_index("cls"), PAIR)


def forward_kernel(
    shifts, bins, class_ids, defocus, images, right, left, sent, out, pictures, moved, spectra, trig, sems, out_sems
):
    def picture_copy(g):
        part = pl.ds(g * GROUP, GROUP)
        return pltpu.make_async_copy(images.at[part], pictures.at[part], sems.at[g])

    for g in range(STACK // GROUP):
        picture_copy(g).start()

    lane = lax.broadcasted_iota(jnp.int32, (SIDE, SIDE), 1)
    line = lax.broadcasted_iota(jnp.int32, (SIDE, SIDE), 0)

    def squared(index):
        signed = jnp.where(index < SIDE // 2, index, index - SIDE).astype(jnp.float32) * (1.0 / SIDE)
        return signed * signed

    by_lane = jnp.zeros((1, SIDE), jnp.float32)
    by_line = jnp.zeros((BINS, SIDE), jnp.float32)
    for b in range(BINS):
        level = defocus[b]
        by_lane = jnp.where(lane[:1] == b, level, by_lane)
        by_line = jnp.where(line[:BINS] == b, level, by_line)
    angles = jnp.concatenate(
        [squared(line) * by_lane + PHASE, squared(lane[:BINS]) * by_line], axis=0
    )
    trig[0] = jnp.sin(angles)
    trig[1] = jnp.cos(angles)

    tag_class = jnp.zeros((1, SIDE), jnp.int32)
    tag_bin = jnp.zeros((1, SIDE), jnp.int32)
    first = lax.rem(member_index(), SIDE // STACK) * STACK
    for p in range(STACK):
        tag_class = jnp.where(lane[:1] == first + p, class_ids[p], tag_class)
        tag_bin = jnp.where(lane[:1] == first + p, bins[p], tag_bin)
    tile = jnp.where(line[:TAGS] == 0, tag_class, jnp.where(line[:TAGS] == 1, tag_bin, 0))
    tile = tile.astype(jnp.float32).astype(jnp.bfloat16)
    for m in range(TEAM):
        out[m, BLOCK:, :] = tile

    def group(g, carry):
        picture_copy(g).wait()
        shifted = []
        for i in range(GROUP):
            p = g * GROUP + i
            picture = pictures[p].astype(jnp.float32)
            picture = pltpu.roll(picture, lax.rem(shifts[1, p] + SIDE, SIDE), axis=1)
            moved[i, REACH : REACH + SIDE, :] = picture
            moved[i, :REACH, :] = picture[SIDE - REACH :]
            moved[i, REACH + SIDE :, :] = picture[:REACH]
            shifted.append(moved[i, pl.ds(REACH - shifts[0, p], SIDE), :].astype(jnp.bfloat16))
        halves = jnp.dot(
            jnp.concatenate(shifted, axis=0), right[...], preferred_element_type=jnp.float32
        ).astype(jnp.bfloat16)
        for i in range(0, GROUP, 2):
            one = halves[i * SIDE : (i + 1) * SIDE]
            two = halves[(i + 1) * SIDE : (i + 2) * SIDE]
            both = jnp.concatenate(
                [
                    jnp.concatenate([one[:, :SIDE], two[:, :SIDE]], axis=1),
                    jnp.concatenate([one[:, SIDE:], two[:, SIDE:]], axis=1),
                ],
                axis=0,
            )
            spectrum = jnp.dot(left[...], both, preferred_element_type=jnp.float32)
            for k in range(2):
                p = g * GROUP + i + k
                level = bins[p]
                which = jnp.full((SIDE, SIDE), level, jnp.int32)
                sin_u = jnp.take_along_axis(trig[0, :SIDE], which, axis=1)
                cos_u = jnp.take_along_axis(trig[1, :SIDE], which, axis=1)
                sin_v = trig[0, pl.ds(SIDE + level, 1), :]
                cos_v = trig[1, pl.ds(SIDE + level, 1), :]
                ctf = -(sin_u * cos_v + cos_u * sin_v)
                start = pl.multiple_of(p * APART, 8)
                spectra[pl.ds(start, SIDE), :] = ctf * spectrum[:, k * SIDE : (k + 1) * SIDE]
        return carry

    lax.fori_loop(0, STACK // GROUP, group, 0)
    def sent_copy(c):
        part = pl.ds(c * SLAB, SLAB)
        return pltpu.make_async_copy(out.at[part], sent.at[part], out_sems.at[c])

    for c in range(TEAM // SLAB):
        for m in range(c * SLAB, (c + 1) * SLAB):
            for j in range(PER):
                row = spectra[pl.ds(j * TEAM + m, STACK, stride=APART), :]
                out[m, j * STACK : (j + 1) * STACK, :] = row.astype(jnp.bfloat16)
        sent_copy(c).start()
    for c in range(TEAM // SLAB):
        sent_copy(c).wait()


def gather_kernel(arrived, out):
    together = SIDE // STACK
    classes = lax.broadcasted_iota(jnp.int32, (CLASSES, SIDE), 0).astype(jnp.float32)
    levels = (lax.broadcasted_iota(jnp.int32, (SIDE, SIDE), 0) % BINS).astype(jnp.float32)
    picks, lots, blocks = [], [], []
    for g in range(TEAM // together):
        members = range(g * together, (g + 1) * together)
        tag = sum(arrived[s, BLOCK:, :].astype(jnp.float32) for s in members)
        picks.append(jnp.where(classes == tag[0:1, :], 1.0, 0.0).astype(jnp.bfloat16))
        lots.append(jnp.where(levels == tag[1:2, :], 1.0, 0.0).astype(jnp.bfloat16))
        parts = [
            jnp.concatenate([arrived[s, j * STACK : (j + 1) * STACK, :] for s in members], axis=0)
            for j in range(PER)
        ]
        blocks.append(jnp.concatenate(parts, axis=1))
    pick = jnp.concatenate(picks, axis=1)
    sums = jnp.dot(pick, jnp.concatenate(blocks, axis=0), preferred_element_type=jnp.float32)
    counts = lax.dot_general(
        pick,
        jnp.concatenate(lots, axis=1),
        (((1,), (1,)), ((), ())),
        preferred_element_type=jnp.float32,
    )
    counts = counts.reshape(FAR, PAIR, OWNED, SIDE)
    lanes = lax.broadcasted_iota(jnp.int32, (FAR, OWNED, SIDE), 2)
    counts = jnp.where(lanes < SIDE // 2, counts[:, 0], counts[:, 1])
    high = jnp.floor(counts * (1.0 / 32.0))
    digits = jnp.where(lanes % (2 * BINS) < BINS, counts - 32.0 * high, high)
    sums = sums.astype(jnp.bfloat16)
    digits = digits.astype(jnp.bfloat16)
    for t in range(FAR):
        far = ORDER[t]
        for j in range(PER):
            out[t, j * NEAR : (j + 1) * NEAR, :] = sums[
                far * NEAR : (far + 1) * NEAR, j * SIDE : (j + 1) * SIDE
            ]
        out[t, PER * NEAR :, :] = digits[far]


def average_kernel(arrived, squares, regular, out):
    total = arrived[0].astype(jnp.float32)
    for z in range(1, FAR):
        total += arrived[z].astype(jnp.float32)
    lanes = lax.broadcasted_iota(jnp.int32, (OWNED, SIDE), 1)
    even = lanes % (2 * BINS) < BINS
    digits = total[PER * NEAR :]
    ahead = pltpu.roll(digits, SIDE - BINS, axis=1)
    behind = pltpu.roll(digits, BINS, axis=1)
    counts = jnp.where(even, digits + 32.0 * ahead, behind + 32.0 * digits)
    other = pltpu.roll(counts, SIDE // 2, axis=1)
    near = lanes < SIDE // 2
    counts = jnp.concatenate(
        [jnp.where(near, counts, other), jnp.where(near, other, counts)], axis=0
    )
    even = jnp.concatenate([even, even], axis=0)
    high = jnp.floor(counts * (1.0 / 128.0))
    digits = jnp.where(even, counts - 128.0 * high, high).astype(jnp.bfloat16)
    denominator = jnp.dot(digits, squares[...], preferred_element_type=jnp.float32)
    denominator = denominator + regular[...]
    averages = [
        (
            total[j * NEAR : (j + 1) * NEAR] / denominator[:, j * SIDE : (j + 1) * SIDE]
        ).astype(jnp.bfloat16)
        for j in range(PER)
    ]
    for i in range(PAIR):
        block = jnp.concatenate(
            [average[i * OWNED : (i + 1) * OWNED] for average in averages], axis=0
        )
        for d in range(N_DOM):
            out[d * PAIR + i] = block


def invert_kernel(arrived, left, right, result, out, rows, sems):
    count = PER * OWNED
    for q in range(TEAM):
        m = (q + (LAST - START) * PAIR) % TEAM
        rows[m * SPREAD : m * SPREAD + count, :] = arrived[q].astype(jnp.float32)

    def picture(k):
        parts = [rows[pl.ds(j * OWNED + k, TEAM, stride=SPREAD), :] for j in range(PER)]
        return jnp.concatenate(parts, axis=0).astype(jnp.bfloat16)

    def result_copy(k):
        part = pl.ds(k, 2)
        return pltpu.make_async_copy(out.at[part], result.at[part], sems.at[k // 2])

    for k in range(0, OWNED, 2):
        both = jnp.concatenate([picture(k), picture(k + 1)], axis=1)
        first = jnp.dot(
            left[...], jnp.concatenate([both, both], axis=0), preferred_element_type=jnp.float32
        ).astype(jnp.bfloat16)
        wide = jnp.concatenate(
            [
                jnp.concatenate([first[:SIDE, :SIDE], first[SIDE:, :SIDE]], axis=1),
                jnp.concatenate([first[:SIDE, SIDE:], first[SIDE:, SIDE:]], axis=1),
            ],
            axis=0,
        )
        pair = jnp.dot(wide, right[...], preferred_element_type=jnp.float32)
        for i in range(2):
            real = pair[i * SIDE : (i + 1) * SIDE]
            power = jnp.sum(real * real, axis=0, keepdims=True)
            power = jnp.sum(power, axis=1, keepdims=True) * (1.0 / (SIDE * SIDE))
            out[k + i] = real * (1.0 / jnp.sqrt(power + EPSILON))
        result_copy(k).start()
    for k in range(0, OWNED, 2):
        result_copy(k).wait()


def teams(start):
    return [
        [(d + start) % N_DOM * N_CLS + t * PAIR + i for d in range(N_DOM) for i in range(PAIR)]
        for t in range(FAR)
    ]


LINES = [[i + PAIR * t for t in ORDER] for i in range(PAIR)]


def exchange(array, axes, groups):
    return lax.all_to_all(
        array, axes, split_axis=0, concat_axis=0, tiled=True, axis_index_groups=groups
    )


def body(images, class_ids, shifts, defocus_bins, defocus, regular):
    member = member_index()
    indices = np.arange(SIDE)
    signed = np.where(indices < SIDE // 2, indices, indices - SIDE).astype(np.float32) / SIDE
    squared = jnp.asarray((signed * signed).astype(np.float32))
    along = defocus[:, None] * squared[None, :]
    sin_u, cos_u = jnp.sin(along + PHASE), jnp.cos(along + PHASE)
    sin_v, cos_v = jnp.sin(along), jnp.cos(along)

    def own(table):
        return lax.dynamic_slice_in_dim(
            table.reshape(*table.shape[:-1], PER, TEAM), member, 1, axis=-1
        )

    mine = own(sin_u) * cos_v[:, None, :] + own(cos_u) * sin_v[:, None, :]
    mine = (mine * mine).reshape(BINS, WIDE)
    high = mine.astype(jnp.bfloat16)
    low = (mine - high.astype(jnp.float32)).astype(jnp.bfloat16)
    squares = jnp.concatenate([high, 128 * high, low, 128 * low], axis=0)
    own_regular = lax.dynamic_slice_in_dim(
        regular.reshape(PER, TEAM, SIDE), member, 1, axis=1
    ).reshape(1, WIDE)

    right, left = forward_tables()
    payload = pl.pallas_call(
        forward_kernel,
        out_shape=jax.ShapeDtypeStruct((TEAM, BLOCK + TAGS, SIDE), jnp.bfloat16),
        in_specs=[SMEM, SMEM, SMEM, SMEM, HBM, VMEM, VMEM],
        out_specs=HBM,
        scratch_shapes=[
            pltpu.VMEM((TEAM, BLOCK + TAGS, SIDE), jnp.bfloat16),
            pltpu.VMEM((STACK, SIDE, SIDE), jnp.bfloat16),
            pltpu.VMEM((GROUP, SIDE + 2 * REACH, SIDE), jnp.float32),
            pltpu.VMEM(((STACK + 1) * APART, SIDE), jnp.float32),
            pltpu.VMEM((2, SIDE + BINS, SIDE), jnp.float32),
            pltpu.SemaphoreType.DMA((STACK // GROUP,)),
            pltpu.SemaphoreType.DMA((TEAM // SLAB,)),
        ],
        compiler_params=ALL,
    )(shifts.T, defocus_bins, class_ids, defocus, images, jnp.asarray(right), jnp.asarray(left))

    arrived = exchange(payload, ("dom", "cls"), teams(START))
    sums = pl.pallas_call(
        gather_kernel,
        out_shape=jax.ShapeDtypeStruct((FAR, PER * NEAR + OWNED, SIDE), jnp.bfloat16),
        in_specs=[VMEM],
        out_specs=VMEM,
        compiler_params=PARAMS,
    )(arrived)

    arrived = exchange(sums, "cls", LINES)
    averages = pl.pallas_call(
        average_kernel,
        out_shape=jax.ShapeDtypeStruct((TEAM, PER * OWNED, SIDE), jnp.bfloat16),
        in_specs=[VMEM, VMEM, VMEM],
        out_specs=VMEM,
        compiler_params=PARAMS,
    )(arrived, squares, own_regular)

    arrived = exchange(averages, ("dom", "cls"), teams(LAST))
    left, right, _ = inverse_tables()
    return pl.pallas_call(
        invert_kernel,
        out_shape=jax.ShapeDtypeStruct((OWNED, SIDE, SIDE), jnp.float32),
        in_specs=[VMEM, VMEM, VMEM],
        out_specs=HBM,
        scratch_shapes=[
            pltpu.VMEM((OWNED, SIDE, SIDE), jnp.float32),
            pltpu.VMEM(((TEAM + 1) * SPREAD, SIDE), jnp.float32),
            pltpu.SemaphoreType.DMA((OWNED // 2,)),
        ],
        compiler_params=PARAMS,
    )(arrived, jnp.asarray(left), jnp.asarray(right))


def solution(mesh):
    in_specs = (
        P(("dom", "cls"), None, None),
        P(("dom", "cls")),
        P(("dom", "cls"), None),
        P(("dom", "cls")),
        P(),
        P(),
    )
    return jax.shard_map(
        body, mesh=mesh, in_specs=in_specs, out_specs=P("cls", None, None), check_vma=False
    )
```

```python
import math

import jax
import jax.numpy as jnp
import ml_dtypes
import numpy as np
from jax import lax
from jax.experimental import pallas as pl
from jax.experimental.pallas import tpu as pltpu
from jax.sharding import PartitionSpec as P

SIDE = 128
STACK = 32
OWNED = 16
CLASSES = 256
N_DOM = 32
N_CLS = 16
BINS = 32
REACH = 16
PAIR = 2
TEAM = N_DOM * PAIR
FAR = N_CLS // PAIR
NEAR = OWNED * PAIR
PER = SIDE // TEAM
BLOCK = PER * STACK
TAGS = 8
ORDER = (5, 1, 6, 2, 7, 3, 0, 4)
STRIDE = 13
FOLD = 4
HEAD = 42
WIDE = PER * SIDE
GROUP = 16
SLAB = 8
LOT = 8
APART = SIDE + 8
SPREAD = PER * OWNED + 8
PHASE = 0.1
EPSILON = 1e-05

VMEM = pl.BlockSpec(memory_space=pltpu.VMEM)
HBM = pl.BlockSpec(memory_space=pl.ANY)
SMEM = pl.BlockSpec(memory_space=pltpu.SMEM)
ALL = pltpu.CompilerParams(vmem_limit_bytes=60 * 1024 * 1024)
PARAMS = pltpu.CompilerParams(vmem_limit_bytes=16 * 1024 * 1024)


def hartley_tables():
    indices = np.arange(SIDE)
    angles = ((indices[:, None] * indices[None, :]) % SIDE).astype(np.float32)
    angles = angles * np.float32(2.0 * math.pi / SIDE)
    return np.cos(angles).astype(np.float32), np.sin(angles).astype(np.float32)


def forward_tables():
    cosine, sine = hartley_tables()
    factor = np.float32(1.0 / math.sqrt(SIDE))
    right = (np.concatenate([cosine + sine, cosine - sine], axis=1) * factor).astype(ml_dtypes.bfloat16)
    left = (np.concatenate([cosine, sine], axis=1) * factor).astype(ml_dtypes.bfloat16)
    return right, left


def split(table):
    high = table.astype(ml_dtypes.bfloat16)
    low = (table - high.astype(np.float32)).astype(ml_dtypes.bfloat16)
    return high, low


def inverse_tables():
    cosine, sine = hartley_tables()
    left_high, left_low = split(np.concatenate([cosine, sine], axis=0))
    left = np.concatenate([left_high, left_low], axis=1)
    right_high, right_low = split(np.concatenate([cosine + sine, cosine - sine], axis=0))
    return left, right_high, right_low


def place(device):
    mixed = (device * STRIDE + (TEAM - HEAD) * STRIDE) % TEAM
    return mixed ^ (mixed // FOLD)


def member_index():
    return place(lax.axis_index("dom") * PAIR + lax.rem(lax.axis_index("cls"), PAIR))


def forward_kernel(
    shifts_in, bins_in, class_ids_in, defocus_in, images, right_in, left_in, sent,
    shifts, bins, class_ids, defocus, right, left, out, pictures, moved, spectra, trig,
    in_sems, sems, out_sems,
):
    pairs = [
        (defocus_in, defocus),
        (shifts_in, shifts),
        (bins_in, bins),
        (class_ids_in, class_ids),
        (right_in, right),
        (left_in, left),
    ]
    copies = [pltpu.make_async_copy(a, b, in_sems.at[i]) for i, (a, b) in enumerate(pairs)]

    def picture_copy(c):
        part = pl.ds(c * LOT, LOT)
        return pltpu.make_async_copy(images.at[part], pictures.at[part], sems.at[c])

    for copy in copies:
        copy.start()
    for c in range(STACK // LOT):
        picture_copy(c).start()
    for copy in copies[:4]:
        copy.wait()

    lane = lax.broadcasted_iota(jnp.int32, (SIDE, SIDE), 1)
    line = lax.broadcasted_iota(jnp.int32, (SIDE, SIDE), 0)

    def squared(index):
        signed = jnp.where(index < SIDE // 2, index, index - SIDE).astype(jnp.float32) * (1.0 / SIDE)
        return signed * signed

    by_lane = jnp.zeros((1, SIDE), jnp.float32)
    by_line = jnp.zeros((BINS, SIDE), jnp.float32)
    for b in range(BINS):
        level = defocus[b]
        by_lane = jnp.where(lane[:1] == b, level, by_lane)
        by_line = jnp.where(line[:BINS] == b, level, by_line)
    angles = jnp.concatenate(
        [squared(line) * by_lane + PHASE, squared(lane[:BINS]) * by_line], axis=0
    )
    trig[0] = jnp.sin(angles)
    trig[1] = jnp.cos(angles)

    tag_class = jnp.zeros((1, SIDE), jnp.int32)
    tag_bin = jnp.zeros((1, SIDE), jnp.int32)
    first = lax.rem(member_index(), SIDE // STACK) * STACK
    for p in range(STACK):
        tag_class = jnp.where(lane[:1] == first + p, class_ids[p], tag_class)
        tag_bin = jnp.where(lane[:1] == first + p, bins[p], tag_bin)
    tile = jnp.where(line[:TAGS] == 0, tag_class, jnp.where(line[:TAGS] == 1, tag_bin, 0))
    tile = tile.astype(jnp.float32).astype(jnp.bfloat16)
    for m in range(TEAM):
        out[m, BLOCK:, :] = tile

    for copy in copies[4:]:
        copy.wait()

    def group(g, carry):
        for c in range(GROUP // LOT):
            picture_copy(g * (GROUP // LOT) + c).wait()
        shifted = []
        for i in range(GROUP):
            p = g * GROUP + i
            picture = pictures[p].astype(jnp.float32)
            picture = pltpu.roll(picture, lax.rem(shifts[1, p] + SIDE, SIDE), axis=1)
            moved[i, REACH : REACH + SIDE, :] = picture
            moved[i, :REACH, :] = picture[SIDE - REACH :]
            moved[i, REACH + SIDE :, :] = picture[:REACH]
            shifted.append(moved[i, pl.ds(REACH - shifts[0, p], SIDE), :].astype(jnp.bfloat16))
        halves = jnp.dot(
            jnp.concatenate(shifted, axis=0), right[...], preferred_element_type=jnp.float32
        ).astype(jnp.bfloat16)
        for i in range(0, GROUP, 2):
            one = halves[i * SIDE : (i + 1) * SIDE]
            two = halves[(i + 1) * SIDE : (i + 2) * SIDE]
            both = jnp.concatenate(
                [
                    jnp.concatenate([one[:, :SIDE], two[:, :SIDE]], axis=1),
                    jnp.concatenate([one[:, SIDE:], two[:, SIDE:]], axis=1),
                ],
                axis=0,
            )
            spectrum = jnp.dot(left[...], both, preferred_element_type=jnp.float32)
            for k in range(2):
                p = g * GROUP + i + k
                level = bins[p]
                which = jnp.full((SIDE, SIDE), level, jnp.int32)
                sin_u = jnp.take_along_axis(trig[0, :SIDE], which, axis=1)
                cos_u = jnp.take_along_axis(trig[1, :SIDE], which, axis=1)
                sin_v = trig[0, pl.ds(SIDE + level, 1), :]
                cos_v = trig[1, pl.ds(SIDE + level, 1), :]
                ctf = -(sin_u * cos_v + cos_u * sin_v)
                start = pl.multiple_of(p * APART, 8)
                spectra[pl.ds(start, SIDE), :] = ctf * spectrum[:, k * SIDE : (k + 1) * SIDE]
        return carry

    lax.fori_loop(0, STACK // GROUP, group, 0)
    def sent_copy(c):
        part = pl.ds(c * SLAB, SLAB)
        return pltpu.make_async_copy(out.at[part], sent.at[part], out_sems.at[c])

    for c in range(TEAM // SLAB):
        for m in range(c * SLAB, (c + 1) * SLAB):
            for j in range(PER):
                row = spectra[pl.ds(j * TEAM + m, STACK, stride=APART), :]
                out[m, j * STACK : (j + 1) * STACK, :] = row.astype(jnp.bfloat16)
        sent_copy(c).start()
    for c in range(TEAM // SLAB):
        sent_copy(c).wait()


def gather_kernel(arrived, out):
    together = SIDE // STACK
    classes = lax.broadcasted_iota(jnp.int32, (CLASSES, SIDE), 0).astype(jnp.float32)
    levels = (lax.broadcasted_iota(jnp.int32, (SIDE, SIDE), 0) % BINS).astype(jnp.float32)
    picks, lots, blocks = [], [], []
    for g in range(TEAM // together):
        members = range(g * together, (g + 1) * together)
        tag = sum(arrived[s, BLOCK:, :].astype(jnp.float32) for s in members)
        picks.append(jnp.where(classes == tag[0:1, :], 1.0, 0.0).astype(jnp.bfloat16))
        lots.append(jnp.where(levels == tag[1:2, :], 1.0, 0.0).astype(jnp.bfloat16))
        parts = [
            jnp.concatenate([arrived[s, j * STACK : (j + 1) * STACK, :] for s in members], axis=0)
            for j in range(PER)
        ]
        blocks.append(jnp.concatenate(parts, axis=1))
    pick = jnp.concatenate(picks, axis=1)
    sums = jnp.dot(pick, jnp.concatenate(blocks, axis=0), preferred_element_type=jnp.float32)
    counts = lax.dot_general(
        pick,
        jnp.concatenate(lots, axis=1),
        (((1,), (1,)), ((), ())),
        preferred_element_type=jnp.float32,
    )
    counts = counts.reshape(FAR, PAIR, OWNED, SIDE)
    lanes = lax.broadcasted_iota(jnp.int32, (FAR, OWNED, SIDE), 2)
    counts = jnp.where(lanes < SIDE // 2, counts[:, 0], counts[:, 1])
    high = jnp.floor(counts * (1.0 / 32.0))
    digits = jnp.where(lanes % (2 * BINS) < BINS, counts - 32.0 * high, high)
    sums = sums.astype(jnp.bfloat16)
    digits = digits.astype(jnp.bfloat16)
    for t in range(FAR):
        far = ORDER[t]
        for j in range(PER):
            out[t, j * NEAR : (j + 1) * NEAR, :] = sums[
                far * NEAR : (far + 1) * NEAR, j * SIDE : (j + 1) * SIDE
            ]
        out[t, PER * NEAR :, :] = digits[far]


def average_kernel(arrived, squares, regular, out):
    total = arrived[0].astype(jnp.float32)
    for z in range(1, FAR):
        total += arrived[z].astype(jnp.float32)
    lanes = lax.broadcasted_iota(jnp.int32, (OWNED, SIDE), 1)
    even = lanes % (2 * BINS) < BINS
    digits = total[PER * NEAR :]
    ahead = pltpu.roll(digits, SIDE - BINS, axis=1)
    behind = pltpu.roll(digits, BINS, axis=1)
    counts = jnp.where(even, digits + 32.0 * ahead, behind + 32.0 * digits)
    other = pltpu.roll(counts, SIDE // 2, axis=1)
    near = lanes < SIDE // 2
    counts = jnp.concatenate(
        [jnp.where(near, counts, other), jnp.where(near, other, counts)], axis=0
    )
    even = jnp.concatenate([even, even], axis=0)
    high = jnp.floor(counts * (1.0 / 128.0))
    digits = jnp.where(even, counts - 128.0 * high, high).astype(jnp.bfloat16)
    denominator = jnp.dot(digits, squares[...], preferred_element_type=jnp.float32)
    denominator = denominator + regular[...]
    averages = [
        (
            total[j * NEAR : (j + 1) * NEAR] / denominator[:, j * SIDE : (j + 1) * SIDE]
        ).astype(jnp.bfloat16)
        for j in range(PER)
    ]
    for i in range(PAIR):
        block = jnp.concatenate(
            [average[i * OWNED : (i + 1) * OWNED] for average in averages], axis=0
        )
        for d in range(N_DOM):
            out[place(d * PAIR + i)] = block


def invert_kernel(arrived, left, right, result, out, rows, sems):
    count = PER * OWNED
    for m in range(TEAM):
        rows[m * SPREAD : m * SPREAD + count, :] = arrived[m].astype(jnp.float32)

    def picture(k):
        parts = [rows[pl.ds(j * OWNED + k, TEAM, stride=SPREAD), :] for j in range(PER)]
        return jnp.concatenate(parts, axis=0).astype(jnp.bfloat16)

    def result_copy(k):
        part = pl.ds(k, 2)
        return pltpu.make_async_copy(out.at[part], result.at[part], sems.at[k // 2])

    for k in range(0, OWNED, 2):
        both = jnp.concatenate([picture(k), picture(k + 1)], axis=1)
        first = jnp.dot(
            left[...], jnp.concatenate([both, both], axis=0), preferred_element_type=jnp.float32
        ).astype(jnp.bfloat16)
        wide = jnp.concatenate(
            [
                jnp.concatenate([first[:SIDE, :SIDE], first[SIDE:, :SIDE]], axis=1),
                jnp.concatenate([first[:SIDE, SIDE:], first[SIDE:, SIDE:]], axis=1),
            ],
            axis=0,
        )
        pair = jnp.dot(wide, right[...], preferred_element_type=jnp.float32)
        for i in range(2):
            real = pair[i * SIDE : (i + 1) * SIDE]
            power = jnp.sum(real * real, axis=0, keepdims=True)
            power = jnp.sum(power, axis=1, keepdims=True) * (1.0 / (SIDE * SIDE))
            out[k + i] = real * (1.0 / jnp.sqrt(power + EPSILON))
        result_copy(k).start()
    for k in range(0, OWNED, 2):
        result_copy(k).wait()


TEAMS = [
    [m // PAIR * N_CLS + t * PAIR + m % PAIR for m in sorted(range(TEAM), key=place)]
    for t in range(FAR)
]
LINES = [[i + PAIR * t for t in ORDER] for i in range(PAIR)]


def exchange(array, axes, groups):
    return lax.all_to_all(
        array, axes, split_axis=0, concat_axis=0, tiled=True, axis_index_groups=groups
    )


def body(images, class_ids, shifts, defocus_bins, defocus, regular):
    member = member_index()
    indices = np.arange(SIDE)
    signed = np.where(indices < SIDE // 2, indices, indices - SIDE).astype(np.float32) / SIDE
    squared = jnp.asarray((signed * signed).astype(np.float32))
    along = defocus[:, None] * squared[None, :]
    sin_u, cos_u = jnp.sin(along + PHASE), jnp.cos(along + PHASE)
    sin_v, cos_v = jnp.sin(along), jnp.cos(along)

    def own(table):
        return lax.dynamic_slice_in_dim(
            table.reshape(*table.shape[:-1], PER, TEAM), member, 1, axis=-1
        )

    mine = own(sin_u) * cos_v[:, None, :] + own(cos_u) * sin_v[:, None, :]
    mine = (mine * mine).reshape(BINS, WIDE)
    high = mine.astype(jnp.bfloat16)
    low = (mine - high.astype(jnp.float32)).astype(jnp.bfloat16)
    squares = jnp.concatenate([high, 128 * high, low, 128 * low], axis=0)
    own_regular = lax.dynamic_slice_in_dim(
        regular.reshape(PER, TEAM, SIDE), member, 1, axis=1
    ).reshape(1, WIDE)

    right, left = forward_tables()
    payload = pl.pallas_call(
        forward_kernel,
        out_shape=jax.ShapeDtypeStruct((TEAM, BLOCK + TAGS, SIDE), jnp.bfloat16),
        in_specs=[HBM] * 7,
        out_specs=HBM,
        scratch_shapes=[
            pltpu.SMEM((2, STACK), jnp.int32),
            pltpu.SMEM((STACK,), jnp.int32),
            pltpu.SMEM((STACK,), jnp.int32),
            pltpu.SMEM((BINS,), jnp.float32),
            pltpu.VMEM((SIDE, 2 * SIDE), jnp.bfloat16),
            pltpu.VMEM((SIDE, 2 * SIDE), jnp.bfloat16),
            pltpu.VMEM((TEAM, BLOCK + TAGS, SIDE), jnp.bfloat16),
            pltpu.VMEM((STACK, SIDE, SIDE), jnp.bfloat16),
            pltpu.VMEM((GROUP, SIDE + 2 * REACH, SIDE), jnp.float32),
            pltpu.VMEM(((STACK + 1) * APART, SIDE), jnp.float32),
            pltpu.VMEM((2, SIDE + BINS, SIDE), jnp.float32),
            pltpu.SemaphoreType.DMA((6,)),
            pltpu.SemaphoreType.DMA((STACK // LOT,)),
            pltpu.SemaphoreType.DMA((TEAM // SLAB,)),
        ],
        compiler_params=ALL,
    )(shifts.T, defocus_bins, class_ids, defocus, images, jnp.asarray(right), jnp.asarray(left))

    arrived = exchange(payload, ("dom", "cls"), TEAMS)
    sums = pl.pallas_call(
        gather_kernel,
        out_shape=jax.ShapeDtypeStruct((FAR, PER * NEAR + OWNED, SIDE), jnp.bfloat16),
        in_specs=[VMEM],
        out_specs=VMEM,
        compiler_params=PARAMS,
    )(arrived)

    arrived = exchange(sums, "cls", LINES)
    averages = pl.pallas_call(
        average_kernel,
        out_shape=jax.ShapeDtypeStruct((TEAM, PER * OWNED, SIDE), jnp.bfloat16),
        in_specs=[VMEM, VMEM, VMEM],
        out_specs=VMEM,
        compiler_params=PARAMS,
    )(arrived, squares, own_regular)

    arrived = exchange(averages, ("dom", "cls"), TEAMS)
    left, right, _ = inverse_tables()
    return pl.pallas_call(
        invert_kernel,
        out_shape=jax.ShapeDtypeStruct((OWNED, SIDE, SIDE), jnp.float32),
        in_specs=[VMEM, VMEM, VMEM],
        out_specs=HBM,
        scratch_shapes=[
            pltpu.VMEM((OWNED, SIDE, SIDE), jnp.float32),
            pltpu.VMEM(((TEAM + 1) * SPREAD, SIDE), jnp.float32),
            pltpu.SemaphoreType.DMA((OWNED // 2,)),
        ],
        compiler_params=PARAMS,
    )(arrived, jnp.asarray(left), jnp.asarray(right))


def solution(mesh):
    in_specs = (
        P(("dom", "cls"), None, None),
        P(("dom", "cls")),
        P(("dom", "cls"), None),
        P(("dom", "cls")),
        P(),
        P(),
    )
    return jax.shard_map(
        body, mesh=mesh, in_specs=in_specs, out_specs=P("cls", None, None), check_vma=False
    )
```

```python
import math

import jax
import jax.numpy as jnp
import ml_dtypes
import numpy as np
from jax import lax
from jax.experimental import pallas as pl
from jax.experimental.pallas import tpu as pltpu
from jax.sharding import PartitionSpec as P

SIDE = 128
STACK = 32
OWNED = 16
CLASSES = 256
N_DOM = 32
N_CLS = 16
BINS = 32
REACH = 16
PAIR = 2
TEAM = N_DOM * PAIR
FAR = N_CLS // PAIR
NEAR = OWNED * PAIR
PER = SIDE // TEAM
BLOCK = PER * STACK
TAGS = 8
LANES = SIDE // BINS
ORDER = (5, 1, 6, 2, 7, 3, 0, 4)
STRIDE = 13
FOLD = 4
HEAD = 42
WIDE = PER * SIDE
GROUP = 16
SLAB = 8
LOT = 8
APART = SIDE + 8
SPREAD = PER * OWNED + 8
PHASE = 0.1
EPSILON = 1e-05

VMEM = pl.BlockSpec(memory_space=pltpu.VMEM)
HBM = pl.BlockSpec(memory_space=pl.ANY)
SMEM = pl.BlockSpec(memory_space=pltpu.SMEM)
ALL = pltpu.CompilerParams(vmem_limit_bytes=60 * 1024 * 1024)
PARAMS = pltpu.CompilerParams(vmem_limit_bytes=16 * 1024 * 1024)


def hartley_tables():
    indices = np.arange(SIDE)
    angles = ((indices[:, None] * indices[None, :]) % SIDE).astype(np.float32)
    angles = angles * np.float32(2.0 * math.pi / SIDE)
    return np.cos(angles).astype(np.float32), np.sin(angles).astype(np.float32)


def forward_tables():
    cosine, sine = hartley_tables()
    factor = np.float32(1.0 / math.sqrt(SIDE))
    right = (np.concatenate([cosine + sine, cosine - sine], axis=1) * factor).astype(ml_dtypes.bfloat16)
    left = (np.concatenate([cosine, sine], axis=1) * factor).astype(ml_dtypes.bfloat16)
    return right, left


def split(table):
    high = table.astype(ml_dtypes.bfloat16)
    low = (table - high.astype(np.float32)).astype(ml_dtypes.bfloat16)
    return high, low


def inverse_tables():
    cosine, sine = hartley_tables()
    left_high, left_low = split(np.concatenate([cosine, sine], axis=0))
    left = np.concatenate([left_high, left_low], axis=1)
    right_high, right_low = split(np.concatenate([cosine + sine, cosine - sine], axis=0))
    return left, right_high, right_low


def place(device):
    mixed = (device * STRIDE + (TEAM - HEAD) * STRIDE) % TEAM
    return mixed ^ (mixed // FOLD)


def member_index():
    return place(lax.axis_index("dom") * PAIR + lax.rem(lax.axis_index("cls"), PAIR))


def forward_kernel(
    shifts_in, bins_in, class_ids_in, defocus_in, images, right_in, left_in, sent,
    shifts, bins, class_ids, defocus, right, left, out, pictures, moved, spectra, trig,
    in_sems, sems, out_sems,
):
    pairs = [
        (defocus_in, defocus),
        (shifts_in, shifts),
        (bins_in, bins),
        (class_ids_in, class_ids),
        (right_in, right),
        (left_in, left),
    ]
    copies = [pltpu.make_async_copy(a, b, in_sems.at[i]) for i, (a, b) in enumerate(pairs)]

    def picture_copy(c):
        part = pl.ds(c * LOT, LOT)
        return pltpu.make_async_copy(images.at[part], pictures.at[part], sems.at[c])

    for copy in copies:
        copy.start()
    for c in range(STACK // LOT):
        picture_copy(c).start()
    for copy in copies[:4]:
        copy.wait()

    lane = lax.broadcasted_iota(jnp.int32, (SIDE, SIDE), 1)
    line = lax.broadcasted_iota(jnp.int32, (SIDE, SIDE), 0)

    def squared(index):
        signed = jnp.where(index < SIDE // 2, index, index - SIDE).astype(jnp.float32) * (1.0 / SIDE)
        return signed * signed

    by_lane = jnp.zeros((1, SIDE), jnp.float32)
    by_line = jnp.zeros((BINS, SIDE), jnp.float32)
    for b in range(BINS):
        level = defocus[b]
        by_lane = jnp.where(lane[:1] == b, level, by_lane)
        by_line = jnp.where(line[:BINS] == b, level, by_line)
    angles = jnp.concatenate(
        [squared(line) * by_lane + PHASE, squared(lane[:BINS]) * by_line], axis=0
    )
    trig[0] = jnp.sin(angles)
    trig[1] = jnp.cos(angles)

    tag_class = jnp.zeros((1, SIDE), jnp.int32)
    tag_bin = jnp.zeros((1, SIDE), jnp.int32)
    first = lax.rem(member_index(), SIDE // STACK) * STACK
    for p in range(STACK):
        tag_class = jnp.where(lane[:1] == first + p, class_ids[p], tag_class)
        tag_bin = jnp.where(lane[:1] == first + p, bins[p], tag_bin)
    tile = jnp.where(line[:TAGS] == 0, tag_class, jnp.where(line[:TAGS] == 1, tag_bin, 0))
    tile = tile.astype(jnp.float32).astype(jnp.bfloat16)
    for m in range(TEAM):
        out[m, BLOCK:, :] = tile

    for copy in copies[4:]:
        copy.wait()

    def group(g, carry):
        for c in range(GROUP // LOT):
            picture_copy(g * (GROUP // LOT) + c).wait()
        shifted = []
        for i in range(GROUP):
            p = g * GROUP + i
            picture = pictures[p].astype(jnp.float32)
            picture = pltpu.roll(picture, lax.rem(shifts[1, p] + SIDE, SIDE), axis=1)
            moved[i, REACH : REACH + SIDE, :] = picture
            moved[i, :REACH, :] = picture[SIDE - REACH :]
            moved[i, REACH + SIDE :, :] = picture[:REACH]
            shifted.append(moved[i, pl.ds(REACH - shifts[0, p], SIDE), :].astype(jnp.bfloat16))
        halves = jnp.dot(
            jnp.concatenate(shifted, axis=0), right[...], preferred_element_type=jnp.float32
        ).astype(jnp.bfloat16)
        for i in range(0, GROUP, 2):
            one = halves[i * SIDE : (i + 1) * SIDE]
            two = halves[(i + 1) * SIDE : (i + 2) * SIDE]
            both = jnp.concatenate(
                [
                    jnp.concatenate([one[:, :SIDE], two[:, :SIDE]], axis=1),
                    jnp.concatenate([one[:, SIDE:], two[:, SIDE:]], axis=1),
                ],
                axis=0,
            )
            spectrum = jnp.dot(left[...], both, preferred_element_type=jnp.float32)
            for k in range(2):
                p = g * GROUP + i + k
                level = bins[p]
                which = jnp.full((SIDE, SIDE), level, jnp.int32)
                sin_u = jnp.take_along_axis(trig[0, :SIDE], which, axis=1)
                cos_u = jnp.take_along_axis(trig[1, :SIDE], which, axis=1)
                sin_v = trig[0, pl.ds(SIDE + level, 1), :]
                cos_v = trig[1, pl.ds(SIDE + level, 1), :]
                ctf = -(sin_u * cos_v + cos_u * sin_v)
                start = pl.multiple_of(p * APART, 8)
                spectra[pl.ds(start, SIDE), :] = ctf * spectrum[:, k * SIDE : (k + 1) * SIDE]
        return carry

    lax.fori_loop(0, STACK // GROUP, group, 0)
    def sent_copy(c):
        part = pl.ds(c * SLAB, SLAB)
        return pltpu.make_async_copy(out.at[part], sent.at[part], out_sems.at[c])

    for c in range(TEAM // SLAB):
        for m in range(c * SLAB, (c + 1) * SLAB):
            for j in range(PER):
                row = spectra[pl.ds(j * TEAM + m, STACK, stride=APART), :]
                out[m, j * STACK : (j + 1) * STACK, :] = row.astype(jnp.bfloat16)
        sent_copy(c).start()
    for c in range(TEAM // SLAB):
        sent_copy(c).wait()


def gather_kernel(arrived, out):
    together = SIDE // STACK
    classes = lax.broadcasted_iota(jnp.int32, (CLASSES, SIDE), 0).astype(jnp.float32)
    levels = (lax.broadcasted_iota(jnp.int32, (SIDE, SIDE), 0) % BINS).astype(jnp.float32)
    picks, lots, blocks = [], [], []
    for g in range(TEAM // together):
        members = range(g * together, (g + 1) * together)
        tag = sum(arrived[s, BLOCK:, :].astype(jnp.float32) for s in members)
        picks.append(jnp.where(classes == tag[0:1, :], 1.0, 0.0).astype(jnp.bfloat16))
        lots.append(jnp.where(levels == tag[1:2, :], 1.0, 0.0).astype(jnp.bfloat16))
        parts = [
            jnp.concatenate([arrived[s, j * STACK : (j + 1) * STACK, :] for s in members], axis=0)
            for j in range(PER)
        ]
        blocks.append(jnp.concatenate(parts, axis=1))
    pick = jnp.concatenate(picks, axis=1)
    sums = jnp.dot(pick, jnp.concatenate(blocks, axis=0), preferred_element_type=jnp.float32)
    counts = lax.dot_general(
        pick,
        jnp.concatenate(lots, axis=1),
        (((1,), (1,)), ((), ())),
        preferred_element_type=jnp.float32,
    )
    counts = counts.reshape(FAR, LANES, TAGS, SIDE)
    lot = lax.broadcasted_iota(jnp.int32, (FAR, TAGS, SIDE), 2) // BINS
    digits = counts[:, 0]
    for i in range(1, LANES):
        digits = jnp.where(lot == i, counts[:, i], digits)
    sums = sums.astype(jnp.bfloat16)
    digits = digits.astype(jnp.bfloat16)
    for t in range(FAR):
        far = ORDER[t]
        for j in range(PER):
            out[t, j * NEAR : (j + 1) * NEAR, :] = sums[
                far * NEAR : (far + 1) * NEAR, j * SIDE : (j + 1) * SIDE
            ]
        out[t, PER * NEAR :, :] = digits[far]


def average_kernel(arrived, squares, regular, out):
    total = arrived[0].astype(jnp.float32)
    for z in range(1, FAR):
        total += arrived[z].astype(jnp.float32)
    lot = lax.broadcasted_iota(jnp.int32, (TAGS, SIDE), 1) // BINS
    parts = []
    for i in range(LANES):
        part = jnp.where(lot == i, total[PER * NEAR :], 0.0)
        part = part + pltpu.roll(part, SIDE // 2, axis=1)
        parts.append(part + pltpu.roll(part, BINS, axis=1))
    counts = jnp.concatenate(parts, axis=0)
    even = lax.broadcasted_iota(jnp.int32, (NEAR, SIDE), 1) % (2 * BINS) < BINS
    high = jnp.floor(counts * (1.0 / 128.0))
    digits = jnp.where(even, counts - 128.0 * high, high).astype(jnp.bfloat16)
    denominator = jnp.dot(digits, squares[...], preferred_element_type=jnp.float32)
    denominator = denominator + regular[...]
    averages = [
        (
            total[j * NEAR : (j + 1) * NEAR] / denominator[:, j * SIDE : (j + 1) * SIDE]
        ).astype(jnp.bfloat16)
        for j in range(PER)
    ]
    for i in range(PAIR):
        block = jnp.concatenate(
            [average[i * OWNED : (i + 1) * OWNED] for average in averages], axis=0
        )
        for d in range(N_DOM):
            out[place(d * PAIR + i)] = block


def invert_kernel(arrived, left, right, result, out, rows, sems):
    count = PER * OWNED
    for m in range(TEAM):
        rows[m * SPREAD : m * SPREAD + count, :] = arrived[m].astype(jnp.float32)

    def picture(k):
        parts = [rows[pl.ds(j * OWNED + k, TEAM, stride=SPREAD), :] for j in range(PER)]
        return jnp.concatenate(parts, axis=0).astype(jnp.bfloat16)

    def result_copy(k):
        part = pl.ds(k, 2)
        return pltpu.make_async_copy(out.at[part], result.at[part], sems.at[k // 2])

    for k in range(0, OWNED, 2):
        both = jnp.concatenate([picture(k), picture(k + 1)], axis=1)
        first = jnp.dot(
            left[...], jnp.concatenate([both, both], axis=0), preferred_element_type=jnp.float32
        ).astype(jnp.bfloat16)
        wide = jnp.concatenate(
            [
                jnp.concatenate([first[:SIDE, :SIDE], first[SIDE:, :SIDE]], axis=1),
                jnp.concatenate([first[:SIDE, SIDE:], first[SIDE:, SIDE:]], axis=1),
            ],
            axis=0,
        )
        pair = jnp.dot(wide, right[...], preferred_element_type=jnp.float32)
        for i in range(2):
            real = pair[i * SIDE : (i + 1) * SIDE]
            power = jnp.sum(real * real, axis=0, keepdims=True)
            power = jnp.sum(power, axis=1, keepdims=True) * (1.0 / (SIDE * SIDE))
            out[k + i] = real * (1.0 / jnp.sqrt(power + EPSILON))
        result_copy(k).start()
    for k in range(0, OWNED, 2):
        result_copy(k).wait()


TEAMS = [
    [m // PAIR * N_CLS + t * PAIR + m % PAIR for m in sorted(range(TEAM), key=place)]
    for t in range(FAR)
]
LINES = [[i + PAIR * t for t in ORDER] for i in range(PAIR)]


def exchange(array, axes, groups):
    return lax.all_to_all(
        array, axes, split_axis=0, concat_axis=0, tiled=True, axis_index_groups=groups
    )


def body(images, class_ids, shifts, defocus_bins, defocus, regular):
    member = member_index()
    indices = np.arange(SIDE)
    signed = np.where(indices < SIDE // 2, indices, indices - SIDE).astype(np.float32) / SIDE
    squared = jnp.asarray((signed * signed).astype(np.float32))
    along = defocus[:, None] * squared[None, :]
    sin_u, cos_u = jnp.sin(along + PHASE), jnp.cos(along + PHASE)
    sin_v, cos_v = jnp.sin(along), jnp.cos(along)

    def own(table):
        return lax.dynamic_slice_in_dim(
            table.reshape(*table.shape[:-1], PER, TEAM), member, 1, axis=-1
        )

    mine = own(sin_u) * cos_v[:, None, :] + own(cos_u) * sin_v[:, None, :]
    mine = (mine * mine).reshape(BINS, WIDE)
    high = mine.astype(jnp.bfloat16)
    low = (mine - high.astype(jnp.float32)).astype(jnp.bfloat16)
    squares = jnp.concatenate([high, 128 * high, low, 128 * low], axis=0)
    own_regular = lax.dynamic_slice_in_dim(
        regular.reshape(PER, TEAM, SIDE), member, 1, axis=1
    ).reshape(1, WIDE)

    right, left = forward_tables()
    payload = pl.pallas_call(
        forward_kernel,
        out_shape=jax.ShapeDtypeStruct((TEAM, BLOCK + TAGS, SIDE), jnp.bfloat16),
        in_specs=[HBM] * 7,
        out_specs=HBM,
        scratch_shapes=[
            pltpu.SMEM((2, STACK), jnp.int32),
            pltpu.SMEM((STACK,), jnp.int32),
            pltpu.SMEM((STACK,), jnp.int32),
            pltpu.SMEM((BINS,), jnp.float32),
            pltpu.VMEM((SIDE, 2 * SIDE), jnp.bfloat16),
            pltpu.VMEM((SIDE, 2 * SIDE), jnp.bfloat16),
            pltpu.VMEM((TEAM, BLOCK + TAGS, SIDE), jnp.bfloat16),
            pltpu.VMEM((STACK, SIDE, SIDE), jnp.bfloat16),
            pltpu.VMEM((GROUP, SIDE + 2 * REACH, SIDE), jnp.float32),
            pltpu.VMEM(((STACK + 1) * APART, SIDE), jnp.float32),
            pltpu.VMEM((2, SIDE + BINS, SIDE), jnp.float32),
            pltpu.SemaphoreType.DMA((6,)),
            pltpu.SemaphoreType.DMA((STACK // LOT,)),
            pltpu.SemaphoreType.DMA((TEAM // SLAB,)),
        ],
        compiler_params=ALL,
    )(shifts.T, defocus_bins, class_ids, defocus, images, jnp.asarray(right), jnp.asarray(left))

    arrived = exchange(payload, ("dom", "cls"), TEAMS)
    sums = pl.pallas_call(
        gather_kernel,
        out_shape=jax.ShapeDtypeStruct((FAR, PER * NEAR + TAGS, SIDE), jnp.bfloat16),
        in_specs=[VMEM],
        out_specs=VMEM,
        compiler_params=PARAMS,
    )(arrived)

    arrived = exchange(sums, "cls", LINES)
    averages = pl.pallas_call(
        average_kernel,
        out_shape=jax.ShapeDtypeStruct((TEAM, PER * OWNED, SIDE), jnp.bfloat16),
        in_specs=[VMEM, VMEM, VMEM],
        out_specs=VMEM,
        compiler_params=PARAMS,
    )(arrived, squares, own_regular)

    arrived = exchange(averages, ("dom", "cls"), TEAMS)
    left, right, _ = inverse_tables()
    return pl.pallas_call(
        invert_kernel,
        out_shape=jax.ShapeDtypeStruct((OWNED, SIDE, SIDE), jnp.float32),
        in_specs=[VMEM, VMEM, VMEM],
        out_specs=HBM,
        scratch_shapes=[
            pltpu.VMEM((OWNED, SIDE, SIDE), jnp.float32),
            pltpu.VMEM(((TEAM + 1) * SPREAD, SIDE), jnp.float32),
            pltpu.SemaphoreType.DMA((OWNED // 2,)),
        ],
        compiler_params=PARAMS,
    )(arrived, jnp.asarray(left), jnp.asarray(right))


def solution(mesh):
    in_specs = (
        P(("dom", "cls"), None, None),
        P(("dom", "cls")),
        P(("dom", "cls"), None),
        P(("dom", "cls")),
        P(),
        P(),
    )
    return jax.shard_map(
        body, mesh=mesh, in_specs=in_specs, out_specs=P("cls", None, None), check_vma=False
    )
```

```python
import math

import jax
import jax.numpy as jnp
import ml_dtypes
import numpy as np
from jax import lax
from jax.experimental import pallas as pl
from jax.experimental.pallas import tpu as pltpu
from jax.sharding import PartitionSpec as P

SIDE = 128
STACK = 32
OWNED = 16
CLASSES = 256
N_DOM = 32
N_CLS = 16
BINS = 32
REACH = 16
PAIR = 2
TEAM = N_DOM * PAIR
FAR = N_CLS // PAIR
NEAR = OWNED * PAIR
PER = SIDE // TEAM
BLOCK = PER * STACK
TAGS = 8
LANES = SIDE // BINS
ORDER = (5, 1, 6, 2, 7, 3, 0, 4)
STRIDE = 13
FOLD = 4
HEAD = 42
WIDE = PER * SIDE
GROUP = 16
SLAB = 8
LOT = 8
APART = SIDE + 8
SPREAD = PER * OWNED + 8
PHASE = 0.1
EPSILON = 1e-05

VMEM = pl.BlockSpec(memory_space=pltpu.VMEM)
HBM = pl.BlockSpec(memory_space=pl.ANY)
SMEM = pl.BlockSpec(memory_space=pltpu.SMEM)
ALL = pltpu.CompilerParams(vmem_limit_bytes=60 * 1024 * 1024)
PARAMS = pltpu.CompilerParams(vmem_limit_bytes=16 * 1024 * 1024)


def hartley_tables():
    indices = np.arange(SIDE)
    angles = ((indices[:, None] * indices[None, :]) % SIDE).astype(np.float32)
    angles = angles * np.float32(2.0 * math.pi / SIDE)
    return np.cos(angles).astype(np.float32), np.sin(angles).astype(np.float32)


def forward_tables():
    cosine, sine = hartley_tables()
    factor = np.float32(1.0 / math.sqrt(SIDE))
    right = (np.concatenate([cosine + sine, cosine - sine], axis=1) * factor).astype(ml_dtypes.bfloat16)
    left = (np.concatenate([cosine, sine], axis=1) * factor).astype(ml_dtypes.bfloat16)
    return right, left


def split(table):
    high = table.astype(ml_dtypes.bfloat16)
    low = (table - high.astype(np.float32)).astype(ml_dtypes.bfloat16)
    return high, low


def inverse_tables():
    cosine, sine = hartley_tables()
    left_high, left_low = split(np.concatenate([cosine, sine], axis=0))
    left = np.concatenate([left_high, left_low], axis=1)
    right_high, right_low = split(np.concatenate([cosine + sine, cosine - sine], axis=0))
    return left, right_high, right_low


def place(device):
    mixed = (device * STRIDE + (TEAM - HEAD) * STRIDE) % TEAM
    return mixed ^ (mixed // FOLD)


def member_index():
    return place(lax.axis_index("dom") * PAIR + lax.rem(lax.axis_index("cls"), PAIR))


def forward_kernel(
    shifts_in, bins_in, class_ids_in, defocus_in, images, right_in, left_in, sent,
    shifts, bins, class_ids, defocus, right, left, out, pictures, moved, spectra, trig,
    in_sems, sems, out_sems,
):
    pairs = [
        (defocus_in, defocus),
        (shifts_in, shifts),
        (bins_in, bins),
        (class_ids_in, class_ids),
        (right_in, right),
        (left_in, left),
    ]
    copies = [pltpu.make_async_copy(a, b, in_sems.at[i]) for i, (a, b) in enumerate(pairs)]

    def picture_copy(c):
        part = pl.ds(c * LOT, LOT)
        return pltpu.make_async_copy(images.at[part], pictures.at[part], sems.at[c])

    for copy in copies[:4]:
        copy.start()
    for c in range(GROUP // LOT):
        picture_copy(c).start()
    for copy in copies[4:]:
        copy.start()
    for c in range(GROUP // LOT, STACK // LOT):
        picture_copy(c).start()
    for copy in copies[:4]:
        copy.wait()

    lane = lax.broadcasted_iota(jnp.int32, (SIDE, SIDE), 1)
    line = lax.broadcasted_iota(jnp.int32, (SIDE, SIDE), 0)

    def squared(index):
        signed = jnp.where(index < SIDE // 2, index, index - SIDE).astype(jnp.float32) * (1.0 / SIDE)
        return signed * signed

    by_lane = jnp.zeros((1, SIDE), jnp.float32)
    by_line = jnp.zeros((BINS, SIDE), jnp.float32)
    for b in range(BINS):
        level = defocus[b]
        by_lane = jnp.where(lane[:1] == b, level, by_lane)
        by_line = jnp.where(line[:BINS] == b, level, by_line)
    angles = jnp.concatenate(
        [squared(line) * by_lane + PHASE, squared(lane[:BINS]) * by_line], axis=0
    )
    trig[0] = jnp.sin(angles)
    trig[1] = jnp.cos(angles)

    tag_class = jnp.zeros((1, SIDE), jnp.int32)
    tag_bin = jnp.zeros((1, SIDE), jnp.int32)
    first = lax.rem(member_index(), SIDE // STACK) * STACK
    for p in range(STACK):
        tag_class = jnp.where(lane[:1] == first + p, class_ids[p], tag_class)
        tag_bin = jnp.where(lane[:1] == first + p, bins[p], tag_bin)
    tile = jnp.where(line[:TAGS] == 0, tag_class, jnp.where(line[:TAGS] == 1, tag_bin, 0))
    tile = tile.astype(jnp.float32).astype(jnp.bfloat16)
    for m in range(TEAM):
        out[m, BLOCK:, :] = tile

    for copy in copies[4:]:
        copy.wait()

    def group(g, carry):
        for c in range(GROUP // LOT):
            picture_copy(g * (GROUP // LOT) + c).wait()
        shifted = []
        for i in range(GROUP):
            p = g * GROUP + i
            picture = pictures[p].astype(jnp.float32)
            picture = pltpu.roll(picture, lax.rem(shifts[1, p] + SIDE, SIDE), axis=1)
            moved[i, REACH : REACH + SIDE, :] = picture
            moved[i, :REACH, :] = picture[SIDE - REACH :]
            moved[i, REACH + SIDE :, :] = picture[:REACH]
            shifted.append(moved[i, pl.ds(REACH - shifts[0, p], SIDE), :].astype(jnp.bfloat16))
        halves = jnp.dot(
            jnp.concatenate(shifted, axis=0), right[...], preferred_element_type=jnp.float32
        ).astype(jnp.bfloat16)
        for i in range(0, GROUP, 2):
            one = halves[i * SIDE : (i + 1) * SIDE]
            two = halves[(i + 1) * SIDE : (i + 2) * SIDE]
            both = jnp.concatenate(
                [
                    jnp.concatenate([one[:, :SIDE], two[:, :SIDE]], axis=1),
                    jnp.concatenate([one[:, SIDE:], two[:, SIDE:]], axis=1),
                ],
                axis=0,
            )
            spectrum = jnp.dot(left[...], both, preferred_element_type=jnp.float32)
            for k in range(2):
                p = g * GROUP + i + k
                level = bins[p]
                which = jnp.full((SIDE, SIDE), level, jnp.int32)
                sin_u = jnp.take_along_axis(trig[0, :SIDE], which, axis=1)
                cos_u = jnp.take_along_axis(trig[1, :SIDE], which, axis=1)
                sin_v = trig[0, pl.ds(SIDE + level, 1), :]
                cos_v = trig[1, pl.ds(SIDE + level, 1), :]
                ctf = -(sin_u * cos_v + cos_u * sin_v)
                start = pl.multiple_of(p * APART, 8)
                spectra[pl.ds(start, SIDE), :] = ctf * spectrum[:, k * SIDE : (k + 1) * SIDE]
        return carry

    lax.fori_loop(0, STACK // GROUP, group, 0)
    def sent_copy(c):
        part = pl.ds(c * SLAB, SLAB)
        return pltpu.make_async_copy(out.at[part], sent.at[part], out_sems.at[c])

    for c in range(TEAM // SLAB):
        for m in range(c * SLAB, (c + 1) * SLAB):
            for j in range(PER):
                row = spectra[pl.ds(j * TEAM + m, STACK, stride=APART), :]
                out[m, j * STACK : (j + 1) * STACK, :] = row.astype(jnp.bfloat16)
        sent_copy(c).start()
    for c in range(TEAM // SLAB):
        sent_copy(c).wait()


def gather_kernel(arrived, out):
    together = SIDE // STACK
    classes = lax.broadcasted_iota(jnp.int32, (CLASSES, SIDE), 0).astype(jnp.float32)
    levels = (lax.broadcasted_iota(jnp.int32, (SIDE, SIDE), 0) % BINS).astype(jnp.float32)
    picks, lots, blocks = [], [], []
    for g in range(TEAM // together):
        members = range(g * together, (g + 1) * together)
        tag = sum(arrived[s, BLOCK:, :].astype(jnp.float32) for s in members)
        picks.append(jnp.where(classes == tag[0:1, :], 1.0, 0.0).astype(jnp.bfloat16))
        lots.append(jnp.where(levels == tag[1:2, :], 1.0, 0.0).astype(jnp.bfloat16))
        parts = [
            jnp.concatenate([arrived[s, j * STACK : (j + 1) * STACK, :] for s in members], axis=0)
            for j in range(PER)
        ]
        blocks.append(jnp.concatenate(parts, axis=1))
    pick = jnp.concatenate(picks, axis=1)
    sums = jnp.dot(pick, jnp.concatenate(blocks, axis=0), preferred_element_type=jnp.float32)
    counts = lax.dot_general(
        pick,
        jnp.concatenate(lots, axis=1),
        (((1,), (1,)), ((), ())),
        preferred_element_type=jnp.float32,
    )
    counts = counts.reshape(FAR, LANES, TAGS, SIDE)
    lot = lax.broadcasted_iota(jnp.int32, (FAR, TAGS, SIDE), 2) // BINS
    digits = counts[:, 0]
    for i in range(1, LANES):
        digits = jnp.where(lot == i, counts[:, i], digits)
    sums = sums.astype(jnp.bfloat16)
    digits = digits.astype(jnp.bfloat16)
    for t in range(FAR):
        far = ORDER[t]
        for j in range(PER):
            out[t, j * NEAR : (j + 1) * NEAR, :] = sums[
                far * NEAR : (far + 1) * NEAR, j * SIDE : (j + 1) * SIDE
            ]
        out[t, PER * NEAR :, :] = digits[far]


def average_kernel(arrived, squares, regular, out):
    total = arrived[0].astype(jnp.float32)
    for z in range(1, FAR):
        total += arrived[z].astype(jnp.float32)
    lot = lax.broadcasted_iota(jnp.int32, (TAGS, SIDE), 1) // BINS
    parts = []
    for i in range(LANES):
        part = jnp.where(lot == i, total[PER * NEAR :], 0.0)
        part = part + pltpu.roll(part, SIDE // 2, axis=1)
        parts.append(part + pltpu.roll(part, BINS, axis=1))
    counts = jnp.concatenate(parts, axis=0)
    even = lax.broadcasted_iota(jnp.int32, (NEAR, SIDE), 1) % (2 * BINS) < BINS
    high = jnp.floor(counts * (1.0 / 128.0))
    digits = jnp.where(even, counts - 128.0 * high, high).astype(jnp.bfloat16)
    denominator = jnp.dot(digits, squares[...], preferred_element_type=jnp.float32)
    denominator = denominator + regular[...]
    averages = [
        (
            total[j * NEAR : (j + 1) * NEAR] / denominator[:, j * SIDE : (j + 1) * SIDE]
        ).astype(jnp.bfloat16)
        for j in range(PER)
    ]
    for i in range(PAIR):
        block = jnp.concatenate(
            [average[i * OWNED : (i + 1) * OWNED] for average in averages], axis=0
        )
        for d in range(N_DOM):
            out[place(d * PAIR + i)] = block


def invert_kernel(arrived, left, right, result, out, rows, sems):
    count = PER * OWNED
    for m in range(TEAM):
        rows[m * SPREAD : m * SPREAD + count, :] = arrived[m].astype(jnp.float32)

    def picture(k):
        parts = [rows[pl.ds(j * OWNED + k, TEAM, stride=SPREAD), :] for j in range(PER)]
        return jnp.concatenate(parts, axis=0).astype(jnp.bfloat16)

    def result_copy(k):
        part = pl.ds(k, 2)
        return pltpu.make_async_copy(out.at[part], result.at[part], sems.at[k // 2])

    for k in range(0, OWNED, 2):
        both = jnp.concatenate([picture(k), picture(k + 1)], axis=1)
        first = jnp.dot(
            left[...], jnp.concatenate([both, both], axis=0), preferred_element_type=jnp.float32
        ).astype(jnp.bfloat16)
        wide = jnp.concatenate(
            [
                jnp.concatenate([first[:SIDE, :SIDE], first[SIDE:, :SIDE]], axis=1),
                jnp.concatenate([first[:SIDE, SIDE:], first[SIDE:, SIDE:]], axis=1),
            ],
            axis=0,
        )
        pair = jnp.dot(wide, right[...], preferred_element_type=jnp.float32)
        for i in range(2):
            real = pair[i * SIDE : (i + 1) * SIDE]
            power = jnp.sum(real * real, axis=0, keepdims=True)
            power = jnp.sum(power, axis=1, keepdims=True) * (1.0 / (SIDE * SIDE))
            out[k + i] = real * (1.0 / jnp.sqrt(power + EPSILON))
        result_copy(k).start()
    for k in range(0, OWNED, 2):
        result_copy(k).wait()


TEAMS = [
    [m // PAIR * N_CLS + t * PAIR + m % PAIR for m in sorted(range(TEAM), key=place)]
    for t in range(FAR)
]
LINES = [[i + PAIR * t for t in ORDER] for i in range(PAIR)]


def exchange(array, axes, groups):
    return lax.all_to_all(
        array, axes, split_axis=0, concat_axis=0, tiled=True, axis_index_groups=groups
    )


def body(images, class_ids, shifts, defocus_bins, defocus, regular):
    member = member_index()
    indices = np.arange(SIDE)
    signed = np.where(indices < SIDE // 2, indices, indices - SIDE).astype(np.float32) / SIDE
    squared = jnp.asarray((signed * signed).astype(np.float32))
    along = defocus[:, None] * squared[None, :]
    sin_u, cos_u = jnp.sin(along + PHASE), jnp.cos(along + PHASE)
    sin_v, cos_v = jnp.sin(along), jnp.cos(along)

    def own(table):
        return lax.dynamic_slice_in_dim(
            table.reshape(*table.shape[:-1], PER, TEAM), member, 1, axis=-1
        )

    mine = own(sin_u) * cos_v[:, None, :] + own(cos_u) * sin_v[:, None, :]
    mine = (mine * mine).reshape(BINS, WIDE)
    high = mine.astype(jnp.bfloat16)
    low = (mine - high.astype(jnp.float32)).astype(jnp.bfloat16)
    squares = jnp.concatenate([high, 128 * high, low, 128 * low], axis=0)
    own_regular = lax.dynamic_slice_in_dim(
        regular.reshape(PER, TEAM, SIDE), member, 1, axis=1
    ).reshape(1, WIDE)

    right, left = forward_tables()
    payload = pl.pallas_call(
        forward_kernel,
        out_shape=jax.ShapeDtypeStruct((TEAM, BLOCK + TAGS, SIDE), jnp.bfloat16),
        in_specs=[HBM] * 7,
        out_specs=HBM,
        scratch_shapes=[
            pltpu.SMEM((2, STACK), jnp.int32),
            pltpu.SMEM((STACK,), jnp.int32),
            pltpu.SMEM((STACK,), jnp.int32),
            pltpu.SMEM((BINS,), jnp.float32),
            pltpu.VMEM((SIDE, 2 * SIDE), jnp.bfloat16),
            pltpu.VMEM((SIDE, 2 * SIDE), jnp.bfloat16),
            pltpu.VMEM((TEAM, BLOCK + TAGS, SIDE), jnp.bfloat16),
            pltpu.VMEM((STACK, SIDE, SIDE), jnp.bfloat16),
            pltpu.VMEM((GROUP, SIDE + 2 * REACH, SIDE), jnp.float32),
            pltpu.VMEM(((STACK + 1) * APART, SIDE), jnp.float32),
            pltpu.VMEM((2, SIDE + BINS, SIDE), jnp.float32),
            pltpu.SemaphoreType.DMA((6,)),
            pltpu.SemaphoreType.DMA((STACK // LOT,)),
            pltpu.SemaphoreType.DMA((TEAM // SLAB,)),
        ],
        compiler_params=ALL,
    )(shifts.T, defocus_bins, class_ids, defocus, images, jnp.asarray(right), jnp.asarray(left))

    arrived = exchange(payload, ("dom", "cls"), TEAMS)
    sums = pl.pallas_call(
        gather_kernel,
        out_shape=jax.ShapeDtypeStruct((FAR, PER * NEAR + TAGS, SIDE), jnp.bfloat16),
        in_specs=[VMEM],
        out_specs=VMEM,
        compiler_params=PARAMS,
    )(arrived)

    arrived = exchange(sums, "cls", LINES)
    averages = pl.pallas_call(
        average_kernel,
        out_shape=jax.ShapeDtypeStruct((TEAM, PER * OWNED, SIDE), jnp.bfloat16),
        in_specs=[VMEM, VMEM, VMEM],
        out_specs=VMEM,
        compiler_params=PARAMS,
    )(arrived, squares, own_regular)

    arrived = exchange(averages, ("dom", "cls"), TEAMS)
    left, right, _ = inverse_tables()
    return pl.pallas_call(
        invert_kernel,
        out_shape=jax.ShapeDtypeStruct((OWNED, SIDE, SIDE), jnp.float32),
        in_specs=[VMEM, VMEM, VMEM],
        out_specs=HBM,
        scratch_shapes=[
            pltpu.VMEM((OWNED, SIDE, SIDE), jnp.float32),
            pltpu.VMEM(((TEAM + 1) * SPREAD, SIDE), jnp.float32),
            pltpu.SemaphoreType.DMA((OWNED // 2,)),
        ],
        compiler_params=PARAMS,
    )(arrived, jnp.asarray(left), jnp.asarray(right))


def solution(mesh):
    in_specs = (
        P(("dom", "cls"), None, None),
        P(("dom", "cls")),
        P(("dom", "cls"), None),
        P(("dom", "cls")),
        P(),
        P(),
    )
    return jax.shard_map(
        body, mesh=mesh, in_specs=in_specs, out_specs=P("cls", None, None), check_vma=False
    )
```
